512 devices in a mesh: ctx: 32 (over x, y, core), head: 16 (over z).
Axes of the slice: x: 4, y: 4, z: 16, core: 2. Of those that a mesh axis runs over, the one named last changes fastest.
Arguments:
- queries: float32 [2048, 128, 576], P('ctx', 'head'), may hold values from -1 to 14
- latent: float32 [16384, 576], P('ctx'), may hold values from -12 to 12
- selected: int32 [32, 32], replicated, may hold values from 0 to 255, as said below
- value_proj: bfloat16 [128, 512, 128], P('head'), may hold values from -2 to 2
- out_proj: bfloat16 [16384, 7168], P('head', 'ctx'), may hold values from -0.046875 to 0.046875
Outputs:
- attn_out: bfloat16 [2048, 7168], P('head', 'ctx')
The draws below stay inside these ranges and needn't reach their ends.
Inputs may be any that keep to these rules, and one draw needn't show every extreme that they name: `selected`: row j lists 32 distinct key-block ids, each at most 224 + j, including that block itself; at most 2 ids of a row lie in one aligned run of 8 blocks (one device's share of the context), and the last row reaches 2.
All inputs are finite; a program needn't handle non-finite values.
Results may differ from the reference program's by a relative error of at most 0.0049.
Values may be sent and summed in bfloat16 or wider, within the bound.
No kernel may reach another device: no remote copies, remote signals or barrier semaphores. Data moves between devices by JAX's collectives and lax.ppermute only.
A program may use at most 128 MiB of HBM per device.

```python
import math
import jax
import jax.numpy as jnp
from jax import lax

D = 7168
LAT = 512
ROPE = 64
VDIM = 128
BLOCK = 64
TOPB = 32
BLK_DEV = 8
HEADS = 128
QUERY_BLOCK_COUNT = 32
QROWS = 2048
KEY_BLOCK_COUNT = 256
CTXLEN = 16384
MOST = 2


def draw_selected(key, part):
    key = jax.random.fold_in(key, 11)
    ordering_score, hot_key = jax.random.split(key)
    owned = KEY_BLOCK_COUNT - QUERY_BLOCK_COUNT + jnp.arange(QUERY_BLOCK_COUNT, dtype=jnp.int32)
    window = owned[:, None] - jnp.arange(MOST, dtype=jnp.int32)[None, :]
    anchor = jnp.zeros((QUERY_BLOCK_COUNT, 1), jnp.int32)
    settled = jnp.concatenate([window, anchor], axis=1)
    block_numbers = jnp.arange(KEY_BLOCK_COUNT, dtype=jnp.int32)
    occupied = jnp.sum((settled[:, :, None] // BLK_DEV == block_numbers[None, None, :] // BLK_DEV).astype(jnp.int32), axis=1)
    eligible = (block_numbers[None, :] >= 1) & (block_numbers[None, :] <= owned[:, None] - MOST)
    hot_runs = jax.random.randint(hot_key, (KEY_BLOCK_COUNT // BLK_DEV,), 0, 6) == 0
    favored_block = jnp.repeat(hot_runs, BLK_DEV).astype(jnp.int32)
    latest_blocks = (block_numbers[None, :] >= owned[:, None] - 63).astype(jnp.int32)
    score_boost = (2 * latest_blocks + favored_block[None, :]) * (1 << 16)
    block_order = (jax.random.randint(ordering_score, (QUERY_BLOCK_COUNT, KEY_BLOCK_COUNT), 0, 1 << 16) + score_boost) * KEY_BLOCK_COUNT + block_numbers[None, :]
    masked = jnp.where(eligible, block_order, -1)
    grouped = masked.reshape(QUERY_BLOCK_COUNT, KEY_BLOCK_COUNT // BLK_DEV, BLK_DEV)
    beaten = jnp.sum((grouped[:, :, None, :] > grouped[:, :, :, None]).astype(jnp.int32), axis=-1).reshape(QUERY_BLOCK_COUNT, KEY_BLOCK_COUNT)
    allowed = eligible & (beaten < MOST - occupied)
    final_rank = jnp.where(allowed, block_order, -1)
    picked = lax.top_k(final_rank, TOPB - MOST - 1)[1].astype(jnp.int32)
    return jnp.concatenate([settled, picked], axis=1)


def draw_latent(key, part):
    key = jax.random.fold_in(key, 23)
    base_key, scale_key = jax.random.split(key)
    row_width = LAT + ROPE
    values = jnp.clip(jax.random.normal(base_key, (CTXLEN, row_width), jnp.float32), -4.0, 4.0)
    scales = jnp.exp(jax.random.uniform(scale_key, (CTXLEN, 1), jnp.float32, math.log(0.3), math.log(3.0)))
    values = values * scales
    return values.astype(jnp.float32)


def draw_queries(key, part):
    key = jax.random.fold_in(key, 37)
    base_key = jax.random.fold_in(key, 0)
    row_width = LAT + ROPE
    array_shape = (QROWS, HEADS, row_width)
    values = 0.1 * jnp.clip(jax.random.normal(base_key, array_shape, jnp.float32), -6.0, 6.0)
    return values.astype(jnp.float32)


def block_scale(own_key, extent, pieces, smallest, largest):
    loudness = 1.0
    for dim, parts in pieces:
        draws = jax.random.uniform(jax.random.fold_in(jax.random.fold_in(own_key, 6), dim), (parts,), jnp.float32, smallest / len(pieces), largest / len(pieces))
        loudness = loudness * jnp.repeat(jnp.exp(draws), extent[dim] // parts).reshape((-1,) + (1,) * (len(extent) - 1 - dim))
    return loudness


def gaussian(own_key, shape, scale, limit, cuts=(), held_as=jnp.bfloat16):
    factor_of = block_scale(own_key, shape, cuts, -0.22, 0.18) if cuts else 1.0
    values = jax.random.normal(own_key, shape, jnp.float32) * scale * factor_of
    return jnp.minimum(jnp.maximum(values, -limit), limit).astype(held_as)


def setup_inputs(seed: int = 0) -> dict:
    keys = jax.random.split(jax.random.key(seed), 6)
    return {
        "queries": draw_queries(jax.random.fold_in(keys[5], 71), 0),
        "latent": draw_latent(jax.random.fold_in(keys[5], 71), 0),
        "selected": draw_selected(jax.random.fold_in(keys[5], 71), 0),
        "value_proj": gaussian(keys[3], (HEADS, LAT, VDIM), (max(1, LAT // 64)) ** -0.5, 2.0, ((0, 16),)),
        "out_proj": gaussian(keys[4], (HEADS * VDIM, D), (HEADS * VDIM) ** -0.5, 0.046875, ((0, 16), (1, 32))),
    }


neg_large = -1.0e30
score_scale = 1.0 / (192.0 ** 0.5)


def reference(queries, latent, selected, value_proj, out_proj):
    row_width = latent.shape[1]
    key_blocks = latent.shape[0] // BLOCK
    cache_blocks = latent.reshape(key_blocks, BLOCK, row_width)
    offsets = jnp.arange(BLOCK, dtype=jnp.int32)
    value_wide = value_proj.astype(jnp.float32)

    def attend_block(block_index):
        chosen = selected[block_index]
        key_rows = cache_blocks[chosen].reshape(TOPB * BLOCK, row_width)
        key_pos = (chosen[:, None] * BLOCK + offsets[None, :]).reshape(TOPB * BLOCK)
        query_pos = (key_blocks - QUERY_BLOCK_COUNT + block_index) * BLOCK + offsets
        visible = key_pos[None, :] <= query_pos[:, None]
        query_rows = lax.dynamic_slice_in_dim(queries, (block_index * BLOCK).astype(jnp.int32), BLOCK, 0)
        scores = jnp.einsum("bhc,kc->bhk", query_rows, key_rows, precision=lax.Precision.HIGHEST) * score_scale
        masked = jnp.where(visible[:, None, :], scores, neg_large)
        row_peak = jnp.max(masked, axis=-1, keepdims=True)
        exponent = jnp.where(visible[:, None, :], jnp.exp(masked - row_peak), 0.0)
        weights = exponent / jnp.sum(exponent, axis=-1, keepdims=True)
        attended = jnp.einsum("bhk,kl->bhl", weights, key_rows[:, :LAT], precision=lax.Precision.HIGHEST)
        head_out = jnp.einsum("bhl,hlv->bhv", attended, value_wide, precision=lax.Precision.HIGHEST).astype(jnp.bfloat16)
        return head_out.reshape(BLOCK, HEADS * VDIM)

    head_all = lax.map(attend_block, jnp.arange(QUERY_BLOCK_COUNT, dtype=jnp.int32)).reshape(QROWS, HEADS * VDIM)
    return jnp.dot(head_all, out_proj, preferred_element_type=jnp.float32).astype(jnp.bfloat16)
```

```python
import functools

import jax
import jax.numpy as jnp
from jax import lax
from jax.experimental import pallas as pl
from jax.experimental.pallas import tpu as pltpu
from jax.sharding import Mesh
from jax.sharding import PartitionSpec as P

NEG = -1e30
SCALE = 1.0 / 192.0**0.5
F32, BF16, S16 = jnp.float32, jnp.bfloat16, jnp.int16
LANES = 128
ZL = 4
LIMIT = 48 * 1024 * 1024


def row_code(peak):
    return jnp.ceil(jnp.log2(jnp.maximum(peak, 1e-30)) * 256.0)


def to_int(x, code):
    y = jnp.round(x * (jnp.exp2(code * (-1.0 / 256.0)) * 32767.0))
    return jnp.clip(y, -32767.0, 32767.0)


def scale_of(code):
    return jnp.exp2(code * (1.0 / 256.0)) * (1.0 / 32767.0)


def as_s16(x):
    return x.astype(jnp.int32).astype(S16)


def as_f32(x):
    return x.astype(jnp.int32).astype(F32)


def lane_ids(shape):
    return lax.broadcasted_iota(jnp.int32, shape, len(shape) - 1)


def dot_nt(a, b):
    return lax.dot_general(a, b, (((1,), (1,)), ((), ())), preferred_element_type=F32)


def dot_nn(a, b):
    return jnp.dot(a, b, preferred_element_type=F32)


def halves(x):
    high = x.astype(BF16)
    return high, (x - high.astype(F32)).astype(BF16)


def parcel_kernel(ids, latent, out, wide, coded, sems):
    blocks, rows, width = latent.shape
    padded = wide.shape[-1]
    for b in range(blocks):
        x = latent[b]
        wide[:, :width] = x
        code = row_code(jnp.max(jnp.abs(x), axis=-1, keepdims=True))
        lanes = lane_ids((rows, padded))
        full = jnp.where(lanes < width, to_int(wide[...], code), code)
        coded[b] = as_s16(full)
    receivers = out.shape[0]
    copies = []
    for d in range(receivers):
        for s in range(2):
            copy = pltpu.make_async_copy(coded.at[ids[d, s]], out.at[d, s], sems.at[2 * d + s])
            copy.start()
            copies.append(copy)
    for copy in copies:
        copy.wait()


def make_parcels(ids, latent, receivers, padded):
    blocks, rows, width = latent.shape
    return pl.pallas_call(
        parcel_kernel,
        out_shape=jax.ShapeDtypeStruct((receivers, 2, rows, padded), S16),
        in_specs=[pl.BlockSpec(memory_space=pltpu.SMEM), pl.BlockSpec(memory_space=pltpu.VMEM)],
        out_specs=pl.BlockSpec(memory_space=pl.ANY),
        scratch_shapes=[
            pltpu.VMEM((rows, padded), F32),
            pltpu.VMEM((blocks, rows, padded), S16),
            pltpu.SemaphoreType.DMA((2 * receivers,)),
        ],
        compiler_params=pltpu.CompilerParams(vmem_limit_bytes=LIMIT),
        cost_estimate=pl.CostEstimate(flops=10**7, bytes_accessed=7 * 10**6, transcendentals=0),
        name="parcels",
    )(ids, latent)


def attend_kernel(places, block_ids, own, q, arrived, value_proj, out, slots, kh_s, kl_s, s_s, sems):
    count = places.shape[0]
    rows, padded = slots.shape[1:]
    heads, lat, vdim = value_proj.shape
    copies = []
    for i in range(count):
        copy = pltpu.make_async_copy(arrived.at[places[i]], slots.at[i], sems.at[i])
        copy.start()
        copies.append(copy)
    width = 576
    lanes = lane_ids((heads * rows, padded))
    qh, ql = halves(jnp.where(lanes < width, q[...], 0.0))
    step = 4
    keys = step * rows
    total = heads * rows
    lane = lane_ids((total, keys))
    row = lax.broadcasted_iota(jnp.int32, (total, keys), 0)
    ahead = lane % rows - row % rows
    which = lane_ids((1, keys)) // rows
    peak = jnp.full((total, 1), NEG, F32)
    for c in range(count // step):
        for i in range(c * step, (c + 1) * step):
            copies[i].wait()
        raw = slots[c * step : (c + 1) * step].reshape(keys, padded)
        wide = as_f32(raw)
        factor = scale_of(wide[:, padded - LANES :])[:, LANES - 1 :]
        kh, kl = halves(wide * factor)
        span = pl.ds(c * keys, keys)
        kh_s[span, :] = kh
        kl_s[span, :] = kl
        s = dot_nt(qh, kh) + dot_nt(ql, kh) + dot_nt(qh, kl)
        room = jnp.zeros((1, keys), jnp.int32)
        for i in range(step):
            room = jnp.where(which == i, (own[0] - block_ids[c * step + i]) * rows, room)
        s = jnp.where(ahead <= room, s, NEG)
        s_s[:, span] = s
        peak = jnp.maximum(peak, jnp.max(s, axis=-1, keepdims=True))
    acc = jnp.zeros((total, lat), F32)
    norm = jnp.zeros((total, 1), F32)
    for c in range(count // step):
        span = pl.ds(c * keys, keys)
        p = jnp.exp((s_s[:, span] - peak) * SCALE)
        norm = norm + jnp.sum(p, axis=-1, keepdims=True)
        ph, plo = halves(p)
        vh = kh_s[span, :lat]
        acc = acc + dot_nn(ph, vh) + dot_nn(plo, vh) + dot_nn(ph, kl_s[span, :lat])
    ah, al = halves(acc / norm)
    pieces = []
    for h in range(heads):
        part = slice(h * rows, (h + 1) * rows)
        pieces.append(dot_nn(ah[part], value_proj[h]) + dot_nn(al[part], value_proj[h]))
    head_out = jnp.concatenate(pieces, axis=-1).astype(BF16).astype(F32)
    code = row_code(jnp.max(jnp.abs(head_out), axis=-1, keepdims=True))
    out[:, : heads * vdim] = as_s16(to_int(head_out, code))
    out[:, heads * vdim :] = as_s16(jnp.broadcast_to(code, (rows, LANES)))


def attend(places, block_ids, own, q, arrived, value_proj):
    count = places.shape[0]
    _, rows, padded = arrived.shape
    heads, lat, vdim = value_proj.shape
    smem = pl.BlockSpec(memory_space=pltpu.SMEM)
    vmem = pl.BlockSpec(memory_space=pltpu.VMEM)
    return pl.pallas_call(
        attend_kernel,
        out_shape=jax.ShapeDtypeStruct((rows, heads * vdim + LANES), S16),
        in_specs=[smem, smem, smem, vmem, pl.BlockSpec(memory_space=pl.ANY), vmem],
        out_specs=vmem,
        scratch_shapes=[
            pltpu.VMEM((count, rows, padded), S16),
            pltpu.VMEM((count * rows, padded), BF16),
            pltpu.VMEM((count * rows, padded), BF16),
            pltpu.VMEM((heads * rows, count * rows), F32),
            pltpu.SemaphoreType.DMA((count,)),
        ],
        compiler_params=pltpu.CompilerParams(vmem_limit_bytes=LIMIT),
        cost_estimate=pl.CostEstimate(flops=7 * 10**9, bytes_accessed=8 * 10**6, transcendentals=10**6),
        name="attend",
    )(places, block_ids, own, q, arrived, value_proj)


def project_kernel(rows_in, weights, out, wide):
    chips, groups, rows, padded = rows_in.shape
    inner = padded - LANES
    cores, _, _, columns = weights.shape
    sums = [None] * cores
    for g in range(groups):
        factor = scale_of(as_f32(rows_in[:, g, :, inner:]).reshape(chips * rows, LANES))[:, :1]
        a = as_f32(rows_in[:, g, :, :inner]).reshape(chips * rows, inner)
        a = (a * factor).astype(BF16)
        for k in range(cores):
            term = dot_nn(a, weights[k, g])
            sums[k] = term if g == 0 else sums[k] + term
    for k in range(cores):
        code = row_code(jnp.max(jnp.abs(sums[k]), axis=-1, keepdims=True))
        wide[:, :columns] = sums[k]
        lanes = lane_ids(wide.shape)
        full = jnp.where(lanes < columns, to_int(wide[...], code), code)
        out[k] = as_s16(full).reshape(out.shape[1:])


def project(rows_in, weights):
    chips, groups, rows, padded = rows_in.shape
    cores, _, inner, columns = weights.shape
    vmem = pl.BlockSpec(memory_space=pltpu.VMEM)
    return pl.pallas_call(
        project_kernel,
        out_shape=jax.ShapeDtypeStruct((cores, chips, rows, 2 * LANES), S16),
        in_specs=[vmem, vmem],
        out_specs=vmem,
        scratch_shapes=[pltpu.VMEM((chips * rows, 2 * LANES), F32)],
        compiler_params=pltpu.CompilerParams(vmem_limit_bytes=LIMIT),
        cost_estimate=pl.CostEstimate(flops=10**9, bytes_accessed=7 * 10**6, transcendentals=0),
        name="project",
    )(rows_in, weights)


def add_kernel(parts, out):
    cores, outer, groups, rows, _ = parts.shape
    columns = out.shape[-1]
    for k in range(cores):
        for g in range(groups):
            total = None
            for z in range(outer):
                x = as_f32(parts[k, z, g])
                x = x * scale_of(x[:, LANES:])[:, LANES - 1 :]
                total = x if z == 0 else total + x
            at = (k * groups + g) * rows
            out[at : at + rows, :] = total[:, :columns].astype(BF16)


def add_parts(parts, columns):
    cores, _, groups, rows, _ = parts.shape
    vmem = pl.BlockSpec(memory_space=pltpu.VMEM)
    return pl.pallas_call(
        add_kernel,
        out_shape=jax.ShapeDtypeStruct((cores * groups * rows, columns), BF16),
        in_specs=[vmem],
        out_specs=vmem,
        name="add_parts",
    )(parts)


def on_device(queries, latent, selected, value_proj, out_proj):
    plane = ("x", "y", "core")
    ctx_count = lax.axis_size(plane)
    ctx_index = lax.axis_index(plane)
    block_rows, heads, width = queries.shape
    per_owner = latent.shape[0] // block_rows
    key_blocks = per_owner * ctx_count
    padded = -(-width // LANES) * LANES
    columns = out_proj.shape[1]

    weights = lax.all_gather(out_proj, ("core", "zl"), axis=0, tiled=False)
    weights = weights.reshape(2, ZL, *out_proj.shape)

    offset = selected - ctx_index * per_owner
    mine = (offset >= 0) & (offset < per_owner)
    first = jnp.min(jnp.where(mine, offset, per_owner - 1), axis=1)
    last = jnp.max(jnp.where(mine, offset, 0), axis=1)
    ids = jnp.stack([first, last], axis=1)
    parcels = make_parcels(ids, latent.reshape(per_owner, block_rows, width), ctx_count, padded)
    arrived = lax.all_to_all(parcels, plane, split_axis=0, concat_axis=0, tiled=True)

    own_list = lax.dynamic_slice_in_dim(selected, ctx_index, 1, 0)[0]
    owner = own_list // per_owner
    second = jnp.any((owner[None, :] == owner[:, None]) & (own_list[None, :] < own_list[:, None]), axis=1)
    places = owner * 2 + second.astype(jnp.int32)
    own = (key_blocks - ctx_count + ctx_index)[None].astype(jnp.int32)

    q = jnp.transpose(queries, (1, 0, 2)).reshape(heads * block_rows, width)
    q = jnp.pad(q, ((0, 0), (0, padded - width)))
    head_out = attend(
        places, own_list, own, q, arrived.reshape(2 * ctx_count, block_rows, padded), value_proj
    )

    rows = block_rows // ZL
    traded = lax.all_to_all(
        head_out.reshape(ZL, rows, head_out.shape[1]), "zl", split_axis=0, concat_axis=0, tiled=True
    )
    gathered = lax.all_gather(traded, ("x", "y"), axis=0, tiled=False)
    partial = project(gathered, weights)
    sent = lax.all_to_all(
        partial.reshape(-1, rows, 2 * LANES), ("core", "zh", "zl"), split_axis=0, concat_axis=0, tiled=True
    )
    return add_parts(sent.reshape(2, -1, ZL, rows, 2 * LANES), columns)


def solution(mesh):
    shape = (4, 4, 2, mesh.shape["head"] // ZL, ZL)
    fine = Mesh(mesh.devices.reshape(shape), ("x", "y", "core", "zh", "zl"))
    ctx, head = ("x", "y", "core"), ("zh", "zl")
    in_specs = (
        P(ctx, head, None),
        P(ctx, None),
        P(),
        P(head, None, None),
        P(head, ctx),
    )
    return jax.shard_map(on_device, mesh=fine, in_specs=in_specs, out_specs=P(head, ctx), check_vma=False)
```

```python
import functools
import math

import jax
import jax.numpy as jnp
from jax import lax
from jax.experimental import pallas as pl
from jax.experimental.pallas import tpu as pltpu
from jax.sharding import Mesh
from jax.sharding import PartitionSpec as P

NEG = -1e30
SCALE = 1.0 / 192.0**0.5
LOG2E = math.log2(math.e)
F32, BF16, S16 = jnp.float32, jnp.bfloat16, jnp.int16
LANES = 128
PAIR = 2
LIMIT = 48 * 1024 * 1024
WHOLE = 60 * 1024 * 1024
SMEM = pl.BlockSpec(memory_space=pltpu.SMEM)
VMEM = pl.BlockSpec(memory_space=pltpu.VMEM)
ANY = pl.BlockSpec(memory_space=pl.ANY)
HBM = pl.BlockSpec(memory_space=pltpu.HBM)
PARAMS = pltpu.CompilerParams(vmem_limit_bytes=LIMIT)


def row_code(peak):
    return jnp.ceil(jnp.log2(jnp.maximum(peak, 1e-30)) * 256.0)


def to_int(x, code):
    y = jnp.round(x * (jnp.exp2(code * (-1.0 / 256.0)) * 32767.0))
    return jnp.clip(y, -32767.0, 32767.0)


def scale_of(code):
    return jnp.exp2(code * (1.0 / 256.0)) * (1.0 / 32767.0)


def as_s16(x):
    return x.astype(jnp.int32).astype(S16)


def as_f32(x):
    return x.astype(jnp.int32).astype(F32)


def row_peak(x):
    return jnp.max(jnp.abs(x), axis=-1, keepdims=True)


def lane_ids(shape):
    return lax.broadcasted_iota(jnp.int32, shape, len(shape) - 1)


def dot_nt(a, b):
    return lax.dot_general(a, b, (((1,), (1,)), ((), ())), preferred_element_type=F32)


def dot_nn(a, b):
    return jnp.dot(a, b, preferred_element_type=F32)


def halves(x):
    high = x.astype(BF16)
    return high, (x - high.astype(F32)).astype(BF16)


def cost(flops, nbytes, exps=0):
    return pl.CostEstimate(flops=flops, bytes_accessed=nbytes, transcendentals=exps)


def parcel_kernel(where, selected, latent_t, out, lists, stage, wide, coded, ids_v, ids, in_sems, id_sems, sems):
    width, total = latent_t.shape
    blocks, part, padded = coded.shape
    block = total // blocks
    groups = total // LANES
    fetch = pltpu.make_async_copy(selected, lists, id_sems.at[0])
    fetch.start()
    loads = []
    for n in range(groups):
        columns = pl.ds(n * LANES, LANES)
        load = pltpu.make_async_copy(latent_t.at[:, columns], stage.at[:, columns], in_sems.at[n])
        load.start()
        loads.append(load)
    fetch.wait()
    offset = lists[...] - where[0]
    mine = (offset >= 0) & (offset < blocks)
    first = jnp.min(jnp.where(mine, offset, blocks - 1), axis=1, keepdims=True)
    last = jnp.max(jnp.where(mine, offset, 0), axis=1, keepdims=True)
    ids_v[...] = jnp.where(lane_ids(ids_v.shape) == 0, first, last)
    move = pltpu.make_async_copy(ids_v, ids, id_sems.at[1])
    move.start()
    lanes = lane_ids((part, padded))
    for n in range(groups):
        loads[n].wait()
        wide[:, :width] = stage[:, n * LANES : (n + 1) * LANES].T
        for m in range(LANES // block):
            at = pl.multiple_of(m * block + where[1], part)
            x = jnp.where(lanes < width, wide[pl.ds(at, part), :], 0.0)
            code = row_code(row_peak(x))
            full = jnp.where(lanes < width, to_int(x, code), code)
            coded[n * (LANES // block) + m] = as_s16(full)
    move.wait()
    copies = []
    for d in range(out.shape[0]):
        for s in range(2):
            copy = pltpu.make_async_copy(coded.at[ids[d, s]], out.at[d, s], sems.at[2 * d + s])
            copy.start()
            copies.append(copy)
    for copy in copies:
        copy.wait()


def make_parcels(where, selected, latent_t, blocks, part, padded):
    receivers = selected.shape[0]
    width, total = latent_t.shape
    return pl.pallas_call(
        parcel_kernel,
        out_shape=jax.ShapeDtypeStruct((receivers, 2, part, padded), S16),
        in_specs=[SMEM, HBM, HBM],
        out_specs=HBM,
        scratch_shapes=[
            pltpu.VMEM(selected.shape, jnp.int32),
            pltpu.VMEM((width, total), F32),
            pltpu.VMEM((LANES, padded), F32),
            pltpu.VMEM((blocks, part, padded), S16),
            pltpu.VMEM((receivers, LANES), jnp.int32),
            pltpu.SMEM((receivers, LANES), jnp.int32),
            pltpu.SemaphoreType.DMA((total // LANES,)),
            pltpu.SemaphoreType.DMA((2,)),
            pltpu.SemaphoreType.DMA((2 * receivers,)),
        ],
        compiler_params=pltpu.CompilerParams(vmem_limit_bytes=WHOLE),
        cost_estimate=cost(10**7, 4 * 10**6),
        name="parcels",
    )(where, selected, latent_t)


def pack_kernel(q, out, wide):
    width = q.shape[-1]
    wide[:, :width] = q[...]
    lanes = lane_ids(wide.shape)
    x = jnp.where(lanes < width, wide[...], 0.0)
    code = row_code(row_peak(x))
    out[...] = as_s16(jnp.where(lanes < width, to_int(x, code), code))


def pack_queries(q, padded):
    rows = q.shape[0]
    return pl.pallas_call(
        pack_kernel,
        out_shape=jax.ShapeDtypeStruct((rows, padded), S16),
        in_specs=[VMEM],
        out_specs=VMEM,
        scratch_shapes=[pltpu.VMEM((rows, padded), F32)],
        compiler_params=PARAMS,
        cost_estimate=cost(10**7, 2 * 10**6),
        name="pack_queries",
    )(q)


def split_kernel(core, own, other, out):
    rows, padded = own.shape
    lat = padded - LANES
    half = rows // 2
    rope = lane_ids((half, LANES)) < LANES // 2
    orders = ((own, 0), (own, half), (other, core[0] * half), (other, (1 - core[0]) * half))
    for n, (q, at) in enumerate(orders):
        span = slice(n * half, (n + 1) * half)
        wide = as_f32(q[pl.ds(at if n < 2 else pl.multiple_of(at, half), half), :])
        wide = wide * (scale_of(wide[:, lat:])[:, LANES - 1 :] * (SCALE * LOG2E))
        high, low = halves(wide[:, :lat])
        out[span, :lat] = high
        out[span, lat : 2 * lat] = low
        tail = jnp.where(rope, wide[:, lat:], 0.0)
        high, low = halves(tail)
        both = high.astype(F32) + pltpu.roll(low.astype(F32), LANES // 2, 1)
        out[span, 2 * lat : 2 * lat + LANES] = both.astype(BF16)
        out[span, 2 * lat + LANES :] = high


def split_queries(core, own, other):
    rows, padded = own.shape
    return pl.pallas_call(
        split_kernel,
        out_shape=jax.ShapeDtypeStruct((PAIR * rows, 2 * padded), BF16),
        in_specs=[SMEM, VMEM, VMEM],
        out_specs=VMEM,
        compiler_params=PARAMS,
        cost_estimate=cost(10**7, 4 * 10**6),
        name="split_queries",
    )(core, own, other)


def attend_kernel(
    places, block_ids, own, q, arrived, vp_own, fetched, passed, out, slots, keys_s, sems
):
    count = places.shape[0]
    part, padded = slots.shape[1:]
    heads, lat, vdim = vp_own.shape
    block = out.shape[0]
    keys = count * part
    tile = q.shape[0] // PAIR
    copies = []
    for i in range(count):
        copy = pltpu.make_async_copy(arrived.at[places[i]], slots.at[i], sems.at[i])
        copy.start()
        copies.append(copy)
    some = fetched.shape[0]
    step = 8
    rope = lane_ids((step * part, LANES)) < LANES // 2
    for c in range(count // step):
        for i in range(c * step, (c + 1) * step):
            copies[i].wait()
        wide = as_f32(slots[c * step : (c + 1) * step].reshape(step * part, padded))
        wide = wide * scale_of(wide[:, lat:])[:, LANES - 1 :]
        span = slice(c * step * part, (c + 1) * step * part)
        high, low = halves(wide[:, :lat])
        keys_s[span, :lat] = high
        keys_s[span, lat : 2 * lat] = low
        tail = jnp.where(rope, wide[:, lat:], 0.0)
        keys_s[span, 2 * lat : 2 * lat + LANES] = (tail + pltpu.roll(tail, LANES // 2, 1)).astype(BF16)
        keys_s[span, 2 * lat + LANES :] = halves(tail)[1]
    lane = lane_ids((1, keys))
    room = jnp.zeros((1, keys), jnp.int32)
    for i in range(count):
        room = jnp.where(lane // part == i, (own[0] - block_ids[i]) * block - own[1], room)
    room = room - lane % part
    spot = lax.broadcasted_iota(jnp.int32, (tile, 1), 0) % block
    results, stats = [], []
    for t in range(PAIR):
        span = slice(t * tile, (t + 1) * tile)
        s = (
            dot_nt(q[span, :lat], keys_s[:, :lat])
            + dot_nt(q[span, lat : 2 * lat], keys_s[:, :lat])
            + dot_nt(q[span, :lat], keys_s[:, lat : 2 * lat])
            + dot_nt(q[span, 2 * lat :], keys_s[:, 2 * lat :])
        )
        s = jnp.where(room + spot >= 0, s, NEG)
        peak = jnp.max(s, axis=-1, keepdims=True)
        p = jnp.exp2(s - peak)
        norm = jnp.sum(p, axis=-1, keepdims=True)
        high, low = halves(p)
        mixed = (
            dot_nn(high, keys_s[:, :lat]) + dot_nn(high, keys_s[:, lat : 2 * lat]) + dot_nn(low, keys_s[:, :lat])
        )
        high, low = halves(mixed / norm)
        stats.append(peak + jnp.log2(norm))
        for h in range(heads):
            rows = slice(h * block, (h + 1) * block)
            maps = vp_own[h] if t == 0 else (fetched[h] if h < some else passed[h - some])
            both = dot_nn(jnp.concatenate([high[rows], low[rows]], axis=0), maps)
            results.append(both[:block] + both[block:])
    head_out = jnp.concatenate(results, axis=-1)
    code = row_code(row_peak(head_out))
    inner = head_out.shape[-1]
    coded = as_s16(to_int(head_out, code))
    half = inner // PAIR
    width = some * vdim
    out[:, :half] = coded[:, :half]
    for n, turn in enumerate((own[2], 1 - own[2])):
        at = pl.multiple_of(half + turn * width, width)
        out[:, pl.ds(at, width)] = coded[:, half + n * width : half + (n + 1) * width]
    lane = lane_ids((block, LANES))
    tail = code
    for n in range(PAIR * heads):
        stat = stats[n // heads][(n % heads) * block : (n % heads + 1) * block] * 2.0
        coarse = jnp.floor(stat)
        at = n
        if n >= heads:
            turn = own[2] if n < heads + some else 1 - own[2]
            at = heads + turn * some + n % some
        tail = jnp.where(lane == at, coarse, tail)
        tail = jnp.where(lane == at + PAIR * heads, (stat - coarse) * 32767.0, tail)
    out[:, inner:] = as_s16(tail)


def attend(places, block_ids, own, q, arrived, vp_own, fetched, passed):
    count = places.shape[0]
    _, part, padded = arrived.shape
    heads, _, vdim = vp_own.shape
    block = q.shape[0] // (PAIR * heads)
    return pl.pallas_call(
        attend_kernel,
        out_shape=jax.ShapeDtypeStruct((block, PAIR * heads * vdim + LANES), S16),
        in_specs=[SMEM, SMEM, SMEM, VMEM, HBM, VMEM, VMEM, VMEM],
        out_specs=VMEM,
        scratch_shapes=[
            pltpu.VMEM((count, part, padded), S16),
            pltpu.VMEM((count * part, 2 * padded), BF16),
            pltpu.SemaphoreType.DMA((count,)),
        ],
        compiler_params=PARAMS,
        cost_estimate=cost(7 * 10**9, 8 * 10**6, 10**6),
        name="attend",
    )(places, block_ids, own, q, arrived, vp_own, fetched, passed)


def merge_kernel(parts, out, *, heads):
    sources, rows, padded = parts.shape
    inner = padded - LANES
    vdim = inner // (PAIR * heads)
    tails = [as_f32(parts[n, :, inner:]) for n in range(sources)]
    logs = [(x + pltpu.roll(x, LANES - PAIR * heads, 1) * (1.0 / 32767.0)) * 0.5 for x in tails]
    scales = [scale_of(x)[:, LANES - 1 :] for x in tails]
    merged = []
    for g in range(sources):
        near, far = g, g ^ 1
        a, b = logs[near], pltpu.roll(logs[far], LANES - heads, 1)
        top = jnp.maximum(a, b)
        a, b = jnp.exp2(a - top), jnp.exp2(b - top)
        total = a + b
        a, b = a / total * scales[near], b / total * scales[far]
        for h in range(heads):
            x = as_f32(parts[near, :, h * vdim : (h + 1) * vdim]) * a[:, h : h + 1]
            y = as_f32(parts[far, :, (heads + h) * vdim : (heads + h + 1) * vdim]) * b[:, h : h + 1]
            merged.append((x + y).astype(BF16).astype(F32))
    head_out = jnp.concatenate(merged, axis=-1)
    code = row_code(row_peak(head_out))
    width = head_out.shape[-1]
    out[:, :width] = as_s16(to_int(head_out, code))
    out[:, width:] = as_s16(jnp.broadcast_to(code, (rows, LANES)))


def merge(parts, heads):
    sources, rows, padded = parts.shape
    return pl.pallas_call(
        functools.partial(merge_kernel, heads=heads),
        out_shape=jax.ShapeDtypeStruct((rows, sources * (padded - LANES) // PAIR + LANES), S16),
        in_specs=[VMEM],
        out_specs=VMEM,
        compiler_params=PARAMS,
        cost_estimate=cost(10**6, 5 * 10**5),
        name="merge",
    )(parts)


def project_kernel(place, rows_in, near_own, near_other, far_own, far_other, out, wide):
    chips, rows, padded = rows_in.shape
    inner = padded - LANES
    columns, depth = near_own.shape
    core = place[0]
    factor = scale_of(as_f32(rows_in[:, :, inner:]).reshape(chips * rows, LANES))[:, :1]
    sums = [None, None]
    for n, member in enumerate((place[1], 1 - place[1])):
        at = pl.multiple_of(member * depth, depth)
        a = as_f32(rows_in[:, :, pl.ds(at, depth)]).reshape(chips * rows, depth)
        a = (a * factor).astype(BF16)
        for k, weights in enumerate(((near_own, far_own), (near_other, far_other))[n]):
            term = dot_nt(a, weights[...])
            sums[k] = term if n == 0 else sums[k] + term
    lanes = lane_ids(wide.shape)
    for k, at in enumerate((core, 1 - core)):
        code = row_code(row_peak(sums[k]))
        wide[:, :columns] = sums[k]
        full = jnp.where(lanes < columns, to_int(wide[...], code), code)
        out[at] = as_s16(full).reshape(out.shape[1:])


def project(place, rows_in, near_own, near_other, far_own, far_other):
    chips, rows, _ = rows_in.shape
    return pl.pallas_call(
        project_kernel,
        out_shape=jax.ShapeDtypeStruct((2, chips, rows, 2 * LANES), S16),
        in_specs=[SMEM] + [VMEM] * 5,
        out_specs=VMEM,
        scratch_shapes=[pltpu.VMEM((chips * rows, 2 * LANES), F32)],
        compiler_params=PARAMS,
        cost_estimate=cost(10**9, 7 * 10**6),
        name="project",
    )(place, rows_in, near_own, near_other, far_own, far_other)


def add_kernel(parts, out):
    cores, outer, groups, rows, _ = parts.shape
    pieces = []
    for k in range(cores):
        for g in range(groups):
            total = None
            for z in range(outer):
                x = as_f32(parts[k, z, g])
                x = x * scale_of(x[:, LANES:])[:, LANES - 1 :]
                total = x if z == 0 else total + x
            pieces.append(total)
    full = jnp.concatenate(pieces, axis=0)
    out[...] = full.T[: out.shape[0], :].astype(BF16)


def add_parts(parts, columns):
    cores, _, groups, rows, _ = parts.shape
    return pl.pallas_call(
        add_kernel,
        out_shape=jax.ShapeDtypeStruct((columns, cores * groups * rows), BF16),
        in_specs=[VMEM],
        out_specs=VMEM,
        name="add_parts",
    )(parts)


def on_device(queries, latent, selected, value_proj, out_proj):
    plane = ("x", "y", "core")
    ctx_count = lax.axis_size(plane)
    ctx_index = lax.axis_index(plane)
    core = lax.axis_index("core").astype(jnp.int32)
    member = lax.axis_index("zb").astype(jnp.int32)
    block, heads, width = queries.shape
    per_owner = latent.shape[0] // block
    key_blocks = per_owner * ctx_count
    padded = -(-width // LANES) * LANES
    columns = out_proj.shape[1]
    part = block // PAIR
    swap = [(0, 1), (1, 0)]
    start = member * part

    where = jnp.stack([(ctx_index * per_owner).astype(jnp.int32), start])
    parcels = make_parcels(where, selected, latent.T, per_owner, part, padded)
    parcels, queries, value_near = lax.optimization_barrier((parcels, queries, value_proj))
    arrived = lax.all_to_all(parcels, plane, split_axis=0, concat_axis=0, tiled=True)

    q = jnp.transpose(queries, (1, 0, 2)).reshape(heads * block, width)
    q_own = pack_queries(q, padded)
    q_other = lax.ppermute(q_own, "zb", swap)
    near_own = out_proj.T
    q_other, near_own = lax.optimization_barrier((q_other, near_own))
    near_other = lax.ppermute(near_own, "zb", swap)
    far_own = lax.ppermute(near_own, "core", swap)
    q_split = split_queries(core[None], q_own, q_other)
    q_own, listed = lax.optimization_barrier((q_own, selected))
    own_list = lax.dynamic_slice_in_dim(listed, ctx_index, 1, 0)[0]
    owner = own_list // per_owner
    second = jnp.any((owner[None, :] == owner[:, None]) & (own_list[None, :] < own_list[:, None]), axis=1)
    places = owner * 2 + second.astype(jnp.int32)
    places, value_near = lax.optimization_barrier((places, value_near))
    fetched = lax.ppermute(lax.dynamic_slice_in_dim(value_near, core * (heads // 2), heads // 2, 0), "zb", swap)
    passed = lax.ppermute(fetched, "core", swap)

    own = jnp.stack([(key_blocks - ctx_count + ctx_index).astype(jnp.int32), start, core])
    arrived = arrived.reshape(2 * ctx_count, part, padded)
    halves_out = attend(places, own_list, own, q_split, arrived, value_proj, fetched, passed)

    halves_out, near_other = lax.optimization_barrier((halves_out, near_other))
    far_other = lax.ppermute(near_other, "core", swap)
    traded = lax.all_to_all(
        halves_out.reshape(PAIR, part, halves_out.shape[1]), "zb", split_axis=0, concat_axis=0, tiled=True
    )
    gathered = lax.all_gather(merge(traded, heads), ("x", "y"), axis=0, tiled=False)
    partial = project(jnp.stack([core, member]), gathered, near_own, near_other, far_own, far_other)
    sent = lax.all_to_all(
        partial.reshape(-1, part, 2 * LANES), ("core", "zq", "zb"), split_axis=0, concat_axis=0, tiled=True
    )
    return add_parts(sent.reshape(2, -1, PAIR, part, 2 * LANES), columns).T


def solution(mesh):
    shape = (4, 4, 2, mesh.shape["head"] // PAIR, PAIR)
    fine = Mesh(mesh.devices.reshape(shape), ("x", "y", "core", "zq", "zb"))
    ctx, head = ("x", "y", "core"), ("zq", "zb")
    in_specs = (
        P(ctx, head, None),
        P(ctx, None),
        P(),
        P(head, None, None),
        P(head, ctx),
    )
    return jax.shard_map(on_device, mesh=fine, in_specs=in_specs, out_specs=P(head, ctx), check_vma=False)
```

```python
import functools
import math

import jax
import jax.numpy as jnp
from jax import lax
from jax.experimental import pallas as pl
from jax.experimental.pallas import tpu as pltpu
from jax.sharding import Mesh
from jax.sharding import PartitionSpec as P

NEG = -1e30
SCALE = 1.0 / 192.0**0.5
LOG2E = math.log2(math.e)
F32, BF16, S16 = jnp.float32, jnp.bfloat16, jnp.int16
LANES = 128
PAIR = 2
LIMIT = 24 * 1024 * 1024
WHOLE = 60 * 1024 * 1024
SMEM = pl.BlockSpec(memory_space=pltpu.SMEM)
VMEM = pl.BlockSpec(memory_space=pltpu.VMEM)
ANY = pl.BlockSpec(memory_space=pl.ANY)
HBM = pl.BlockSpec(memory_space=pltpu.HBM)
PARAMS = pltpu.CompilerParams(vmem_limit_bytes=LIMIT)


def row_code(peak):
    return jnp.ceil(jnp.log2(jnp.maximum(peak, 1e-30)) * 256.0)


def to_int(x, code):
    y = jnp.round(x * (jnp.exp2(code * (-1.0 / 256.0)) * 32767.0))
    return jnp.clip(y, -32767.0, 32767.0)


def scale_of(code):
    return jnp.exp2(code * (1.0 / 256.0)) * (1.0 / 32767.0)


def as_s16(x):
    return x.astype(jnp.int32).astype(S16)


def as_f32(x):
    return x.astype(jnp.int32).astype(F32)


def row_peak(x):
    return jnp.max(jnp.abs(x), axis=-1, keepdims=True)


def lane_ids(shape):
    return lax.broadcasted_iota(jnp.int32, shape, len(shape) - 1)


def dot_nt(a, b):
    return lax.dot_general(a, b, (((1,), (1,)), ((), ())), preferred_element_type=F32)


def dot_nn(a, b):
    return jnp.dot(a, b, preferred_element_type=F32)


def halves(x):
    high = x.astype(BF16)
    return high, (x - high.astype(F32)).astype(BF16)


def cost(flops, nbytes, exps=0):
    return pl.CostEstimate(flops=flops, bytes_accessed=nbytes, transcendentals=exps)


def parcel_kernel(where, selected, latent_t, out, lists, stage, wide, coded, ids_v, ids, in_sems, id_sems, sems):
    width, total = latent_t.shape
    blocks, part, padded = coded.shape
    block = total // blocks
    groups = total // LANES
    fetch = pltpu.make_async_copy(selected, lists, id_sems.at[0])
    fetch.start()
    loads = []
    for n in range(groups):
        columns = pl.ds(n * LANES, LANES)
        load = pltpu.make_async_copy(latent_t.at[:, columns], stage.at[:, columns], in_sems.at[n])
        load.start()
        loads.append(load)
    fetch.wait()
    offset = lists[...] - where[0]
    mine = (offset >= 0) & (offset < blocks)
    first = jnp.min(jnp.where(mine, offset, blocks), axis=1, keepdims=True)
    last = jnp.max(jnp.where(mine, offset, -1), axis=1, keepdims=True)
    ids_v[...] = jnp.where(lane_ids(ids_v.shape) == 0, first, last)
    move = pltpu.make_async_copy(ids_v, ids, id_sems.at[1])
    move.start()
    lanes = lane_ids((part, padded))
    for n in range(groups):
        loads[n].wait()
        wide[:, :width] = stage[:, n * LANES : (n + 1) * LANES].T
        for m in range(LANES // block):
            at = pl.multiple_of(m * block + where[1], part)
            x = jnp.where(lanes < width, wide[pl.ds(at, part), :], 0.0)
            code = row_code(row_peak(x))
            full = jnp.where(lanes < width, to_int(x, code), code)
            coded[n * (LANES // block) + m] = as_s16(full)
    move.wait()
    copies = []
    for d in range(out.shape[0]):
        low, high = ids[d, 0], ids[d, 1]
        for s, (block_id, filled) in enumerate(((low, low <= high), (high, low < high))):
            copy = pltpu.make_async_copy(coded.at[jnp.clip(block_id, 0, blocks - 1)], out.at[d, s], sems.at[2 * d + s])
            pl.when(filled)(copy.start)
            copies.append((filled, copy))
    for filled, copy in copies:
        pl.when(filled)(copy.wait)


def make_parcels(where, selected, latent_t, blocks, part, padded):
    receivers = selected.shape[0]
    width, total = latent_t.shape
    return pl.pallas_call(
        parcel_kernel,
        out_shape=jax.ShapeDtypeStruct((receivers, 2, part, padded), S16),
        in_specs=[SMEM, HBM, HBM],
        out_specs=HBM,
        scratch_shapes=[
            pltpu.VMEM(selected.shape, jnp.int32),
            pltpu.VMEM((width, total), F32),
            pltpu.VMEM((LANES, padded), F32),
            pltpu.VMEM((blocks, part, padded), S16),
            pltpu.VMEM((receivers, LANES), jnp.int32),
            pltpu.SMEM((receivers, LANES), jnp.int32),
            pltpu.SemaphoreType.DMA((total // LANES,)),
            pltpu.SemaphoreType.DMA((2,)),
            pltpu.SemaphoreType.DMA((2 * receivers,)),
        ],
        compiler_params=pltpu.CompilerParams(vmem_limit_bytes=WHOLE),
        cost_estimate=cost(10**7, 4 * 10**6),
        name="parcels",
    )(where, selected, latent_t)


def pack_kernel(q, out, wide):
    width = q.shape[-1]
    wide[:, :width] = q[...]
    lanes = lane_ids(wide.shape)
    x = jnp.where(lanes < width, wide[...], 0.0)
    code = row_code(row_peak(x))
    out[...] = as_s16(jnp.where(lanes < width, to_int(x, code), code))


def pack_queries(q, padded):
    rows = q.shape[0]
    return pl.pallas_call(
        pack_kernel,
        out_shape=jax.ShapeDtypeStruct((rows, padded), S16),
        in_specs=[VMEM],
        out_specs=VMEM,
        scratch_shapes=[pltpu.VMEM((rows, padded), F32)],
        compiler_params=PARAMS,
        cost_estimate=cost(10**7, 2 * 10**6),
        name="pack_queries",
    )(q)


def load_queries(place, half, own, other, q_s, heads):
    rows, padded = own.shape
    block = rows // heads
    part = block // PAIR
    some = heads // 2
    lat = padded - LANES
    core, member = place[0], place[1]
    begin = (member if half == 1 else 1 - member) * part
    rope = lane_ids((part, LANES)) < LANES // 2
    for n in range(PAIR * heads):
        head = n
        if n >= heads:
            head = ((n - heads) // some + core) % 2 * some + n % some
        at = pl.multiple_of(head * block + begin, part)
        wide = as_f32((own if n < heads else other)[pl.ds(at, part), :])
        wide = wide * (scale_of(wide[:, lat:])[:, LANES - 1 :] * (SCALE * LOG2E))
        span = slice(n * part, (n + 1) * part)
        high, low = halves(wide[:, :lat])
        q_s[span, :lat] = high
        q_s[span, lat : 2 * lat] = low
        high, low = halves(jnp.where(rope, wide[:, lat:], 0.0))
        both = high.astype(F32) + pltpu.roll(low.astype(F32), LANES // 2, 1)
        q_s[span, 2 * lat : 2 * lat + LANES] = both.astype(BF16)
        q_s[span, 2 * lat + LANES :] = high


def fetch_keys(places, arrived, slots, sems):
    copies = []
    for i in range(places.shape[0]):
        copy = pltpu.make_async_copy(arrived.at[places[i]], slots.at[i], sems.at[i])
        copy.start()
        copies.append(copy)
    return copies


def split_keys(copies, slots, keys_s):
    count, part, padded = slots.shape
    lat = padded - LANES
    step = 8
    rope = lane_ids((step * part, LANES)) < LANES // 2
    for c in range(count // step):
        for i in range(c * step, (c + 1) * step):
            copies[i].wait()
        wide = as_f32(slots[c * step : (c + 1) * step].reshape(step * part, padded))
        wide = wide * scale_of(wide[:, lat:])[:, LANES - 1 :]
        span = slice(c * step * part, (c + 1) * step * part)
        high, low = halves(wide[:, :lat])
        keys_s[span, :lat] = high
        keys_s[span, lat : 2 * lat] = low
        tail = jnp.where(rope, wide[:, lat:], 0.0)
        keys_s[span, 2 * lat : 2 * lat + LANES] = (tail + pltpu.roll(tail, LANES // 2, 1)).astype(BF16)
        keys_s[span, 2 * lat + LANES :] = halves(tail)[1]


def attend_rows(block_ids, place, half, q, keys_s, vp_own, fetched, passed, out):
    heads, lat, vdim = vp_own.shape
    count = block_ids.shape[0]
    part = out.shape[0]
    some = fetched.shape[0]
    keys = keys_s.shape[0]
    lane = lane_ids((1, keys))
    room = jnp.zeros((1, keys), jnp.int32)
    for i in range(count):
        room = jnp.where(lane // part == i, (place[2] - block_ids[i]) * (PAIR * part), room)
    if half == 0:
        room = room + (1 - 2 * place[1]) * part
    room = room - lane % part
    spot = lax.broadcasted_iota(jnp.int32, (q.shape[0], 1), 0) % part
    s = (
        dot_nt(q[:, :lat], keys_s[:, :lat])
        + dot_nt(q[:, lat : 2 * lat], keys_s[:, :lat])
        + dot_nt(q[:, :lat], keys_s[:, lat : 2 * lat])
        + dot_nt(q[:, 2 * lat :], keys_s[:, 2 * lat :])
    )
    s = jnp.where(room + spot >= 0, s, NEG)
    peak = jnp.max(s, axis=-1, keepdims=True)
    p = jnp.exp2(s - peak)
    norm = jnp.sum(p, axis=-1, keepdims=True)
    high, low = halves(p)
    mixed = dot_nn(high, keys_s[:, :lat]) + dot_nn(high, keys_s[:, lat : 2 * lat]) + dot_nn(low, keys_s[:, :lat])
    high, low = halves(mixed / norm)
    stat = (peak + jnp.log2(norm)) * 2.0
    coarse = jnp.floor(stat)
    fine = (stat - coarse) * 32767.0
    results = []
    for n in range(PAIR * heads):
        rows = slice(n * part, (n + 1) * part)
        maps = vp_own[n] if n < heads else (fetched[n - heads] if n < heads + some else passed[n - heads - some])
        both = dot_nn(jnp.concatenate([high[rows], low[rows]], axis=0), maps)
        results.append(both[:part] + both[part:])
    head_out = jnp.concatenate(results, axis=-1)
    code = row_code(row_peak(head_out))
    inner = head_out.shape[-1]
    coded = as_s16(to_int(head_out, code))
    half = inner // PAIR
    width = some * vdim
    out[:, :half] = coded[:, :half]
    for n, turn in enumerate((place[0], 1 - place[0])):
        at = pl.multiple_of(half + turn * width, width)
        out[:, pl.ds(at, width)] = coded[:, half + n * width : half + (n + 1) * width]
    lane = lane_ids((part, LANES))
    tail = code
    for n in range(PAIR * heads):
        rows = slice(n * part, (n + 1) * part)
        at = n
        if n >= heads:
            turn = place[0] if n < heads + some else 1 - place[0]
            at = heads + turn * some + n % some
        tail = jnp.where(lane == at, coarse[rows], tail)
        tail = jnp.where(lane == at + PAIR * heads, fine[rows], tail)
    out[:, inner:] = as_s16(tail)


def far_kernel(
    places, block_ids, place, own, other, arrived, vp_own, fetched, passed, out, keys_s, slots, q_s, sems
):
    copies = fetch_keys(places, arrived, slots, sems)
    load_queries(place, 0, own, other, q_s, vp_own.shape[0])
    split_keys(copies, slots, keys_s)
    attend_rows(block_ids, place, 0, q_s, keys_s, vp_own, fetched, passed, out)


def near_kernel(block_ids, place, own, other, keys_s, vp_own, fetched, passed, out, q_s):
    load_queries(place, 1, own, other, q_s, vp_own.shape[0])
    attend_rows(block_ids, place, 1, q_s, keys_s, vp_own, fetched, passed, out)


def attend_far(places, block_ids, place, own, other, arrived, vp_own, fetched, passed):
    count = places.shape[0]
    _, part, padded = arrived.shape
    heads, _, vdim = vp_own.shape
    return pl.pallas_call(
        far_kernel,
        out_shape=(
            jax.ShapeDtypeStruct((part, PAIR * heads * vdim + LANES), S16),
            jax.ShapeDtypeStruct((count * part, 2 * padded), BF16),
        ),
        in_specs=[SMEM, SMEM, SMEM, VMEM, VMEM, HBM, VMEM, VMEM, VMEM],
        out_specs=(VMEM, VMEM),
        scratch_shapes=[
            pltpu.VMEM((count, part, padded), S16),
            pltpu.VMEM((own.shape[0], 2 * padded), BF16),
            pltpu.SemaphoreType.DMA((count,)),
        ],
        compiler_params=PARAMS,
        cost_estimate=cost(4 * 10**9, 6 * 10**6, 10**6),
        name="attend_far",
    )(places, block_ids, place, own, other, arrived, vp_own, fetched, passed)


def attend_near(block_ids, place, own, other, keys, vp_own, fetched, passed, part):
    heads, _, vdim = vp_own.shape
    return pl.pallas_call(
        near_kernel,
        out_shape=jax.ShapeDtypeStruct((part, PAIR * heads * vdim + LANES), S16),
        in_specs=[SMEM, SMEM, VMEM, VMEM, VMEM, VMEM, VMEM, VMEM],
        out_specs=VMEM,
        scratch_shapes=[pltpu.VMEM((own.shape[0], 2 * own.shape[1]), BF16)],
        compiler_params=PARAMS,
        cost_estimate=cost(4 * 10**9, 6 * 10**6, 10**6),
        name="attend_near",
    )(block_ids, place, own, other, keys, vp_own, fetched, passed)


def merge_kernel(place, here, there, out, *, heads):
    rows, padded = here.shape
    inner = padded - LANES
    width = inner // PAIR
    vdim = width // heads
    tails = [as_f32(x[:, inner:]) for x in (here, there)]
    logs = [(x + pltpu.roll(x, LANES - PAIR * heads, 1) * (1.0 / 32767.0)) * 0.5 for x in tails]
    scales = [scale_of(x)[:, LANES - 1 :] for x in tails]
    merged = []
    for g in range(PAIR):
        a = logs[0] if g == 0 else pltpu.roll(logs[0], LANES - heads, 1)
        b = logs[1] if g == 1 else pltpu.roll(logs[1], LANES - heads, 1)
        top = jnp.maximum(a, b)
        a, b = jnp.exp2(a - top), jnp.exp2(b - top)
        total = a + b
        a, b = a / total * scales[0], b / total * scales[1]
        for h in range(heads):
            x = as_f32(here[:, g * width + h * vdim : g * width + (h + 1) * vdim]) * a[:, h : h + 1]
            y = as_f32(there[:, (1 - g) * width + h * vdim : (1 - g) * width + (h + 1) * vdim]) * b[:, h : h + 1]
            merged.append((x + y).astype(BF16).astype(F32))
    head_out = jnp.concatenate(merged, axis=-1)
    code = row_code(row_peak(head_out))
    coded = as_s16(to_int(head_out, code))
    for g, turn in enumerate((place[1], 1 - place[1])):
        out[:, pl.ds(pl.multiple_of(turn * width, width), width)] = coded[:, g * width : (g + 1) * width]
    out[:, inner:] = as_s16(jnp.broadcast_to(code, (rows, LANES)))


def merge(place, here, there, heads):
    return pl.pallas_call(
        functools.partial(merge_kernel, heads=heads),
        out_shape=jax.ShapeDtypeStruct(here.shape, S16),
        in_specs=[SMEM, VMEM, VMEM],
        out_specs=VMEM,
        compiler_params=PARAMS,
        cost_estimate=cost(10**6, 5 * 10**5),
        name="merge",
    )(place, here, there)


def project_kernel(place, rows_in, near_own, near_other, far_own, far_other, out, wide):
    chips, rows, padded = rows_in.shape
    inner = padded - LANES
    columns, depth = near_own.shape
    core = place[0]
    factor = scale_of(as_f32(rows_in[:, :, inner:]).reshape(chips * rows, LANES))[:, :1]
    sums = [None, None]
    for n, member in enumerate((place[1], 1 - place[1])):
        at = pl.multiple_of(member * depth, depth)
        a = as_f32(rows_in[:, :, pl.ds(at, depth)]).reshape(chips * rows, depth)
        a = (a * factor).astype(BF16)
        for k, weights in enumerate(((near_own, far_own), (near_other, far_other))[n]):
            term = dot_nt(a, weights[...])
            sums[k] = term if n == 0 else sums[k] + term
    spare = 2 * LANES - columns
    keep = LANES - spare
    groups = rows // 8
    for k, at in enumerate((core, 1 - core)):
        wide[:, :columns] = sums[k]
        out[at, :, :rows, :] = wide[:, :LANES].reshape(chips, rows, LANES).astype(BF16)
        rest = wide[:, LANES:].reshape(chips, groups, 8, LANES)
        last = rest[:, groups - 1].reshape(chips * 8, LANES)
        lanes = lane_ids(last.shape)
        packed = []
        for g in range(groups - 1):
            moved = pltpu.roll(last, (keep - spare * g) % LANES, 1)
            packed.append(jnp.where(lanes < keep, rest[:, g].reshape(chips * 8, LANES), moved))
        packed = jnp.concatenate([x.reshape(chips, 8, LANES) for x in packed], axis=1)
        out[at, :, rows:, :] = packed.astype(BF16)


def project(place, rows_in, near_own, near_other, far_own, far_other):
    chips, rows, _ = rows_in.shape
    return pl.pallas_call(
        project_kernel,
        out_shape=jax.ShapeDtypeStruct((2, chips, rows * near_own.shape[0] // LANES, LANES), BF16),
        in_specs=[SMEM] + [VMEM] * 5,
        out_specs=VMEM,
        scratch_shapes=[pltpu.VMEM((chips * rows, 2 * LANES), F32)],
        compiler_params=PARAMS,
        cost_estimate=cost(10**9, 7 * 10**6),
        name="project",
    )(place, rows_in, near_own, near_other, far_own, far_other)


def add_kernel(parts, out):
    cores, outer, groups, packed, _ = parts.shape
    columns, total = out.shape
    rows = total // (cores * groups)
    spare = 2 * LANES - columns
    keep = LANES - spare
    lanes = lane_ids((8, LANES))
    left, right = [], []
    for k in range(cores):
        for g in range(groups):
            full = parts[k, 0, g].astype(F32)
            for z in range(1, outer):
                full = full + parts[k, z, g].astype(F32)
            left.append(full[:rows])
            pieces = [full[rows + 8 * n : rows + 8 * (n + 1)] for n in range(rows // 8 - 1)]
            last = jnp.zeros((8, LANES), F32)
            for n, piece in enumerate(pieces):
                moved = pltpu.roll(piece, (spare * n - keep) % LANES, 1)
                last = jnp.where((lanes >= spare * n) & (lanes < spare * (n + 1)), moved, last)
            right.extend(pieces + [last])
    out[:LANES, :] = jnp.concatenate(left, axis=0).T.astype(BF16)
    out[LANES:, :] = jnp.concatenate(right, axis=0).T[: columns - LANES].astype(BF16)


def add_parts(parts, columns):
    cores, _, groups, packed, _ = parts.shape
    rows = packed * LANES // columns
    return pl.pallas_call(
        add_kernel,
        out_shape=jax.ShapeDtypeStruct((columns, cores * groups * rows), BF16),
        in_specs=[VMEM],
        out_specs=VMEM,
        name="add_parts",
    )(parts)


def on_device(queries, latent, selected, value_proj, out_proj):
    plane = ("x", "y", "core")
    ctx_count = lax.axis_size(plane)
    ctx_index = lax.axis_index(plane)
    core = lax.axis_index("core").astype(jnp.int32)
    member = lax.axis_index("zb").astype(jnp.int32)
    block, heads, width = queries.shape
    per_owner = latent.shape[0] // block
    key_blocks = per_owner * ctx_count
    padded = -(-width // LANES) * LANES
    columns = out_proj.shape[1]
    part = block // PAIR
    swap = [(0, 1), (1, 0)]
    start = member * part

    where = jnp.stack([(ctx_index * per_owner).astype(jnp.int32), start])
    parcels = make_parcels(where, selected, latent.T, per_owner, part, padded)
    parcels, queries, value_near = lax.optimization_barrier((parcels, queries, value_proj))
    arrived = lax.all_to_all(parcels, plane, split_axis=0, concat_axis=0, tiled=True)

    q = jnp.transpose(queries, (1, 0, 2)).reshape(heads * block, width)
    near_own = out_proj.T
    q_own = pack_queries(q, padded)
    q_other = lax.ppermute(q_own, "zb", swap)
    near_own = lax.optimization_barrier((q_own, near_own))[1]
    far_own = lax.ppermute(near_own, "core", swap)
    place = jnp.stack([core, member, key_blocks - ctx_count + ctx_index]).astype(jnp.int32)

    listed = lax.optimization_barrier((q_own, selected))[1]
    own_list = lax.dynamic_slice_in_dim(listed, ctx_index, 1, 0)[0]
    owner = own_list // per_owner
    second = jnp.any((owner[None, :] == owner[:, None]) & (own_list[None, :] < own_list[:, None]), axis=1)
    places = owner * 2 + second.astype(jnp.int32)
    places, value_near = lax.optimization_barrier((places, value_near))
    fetched = lax.ppermute(lax.dynamic_slice_in_dim(value_near, core * (heads // 2), heads // 2, 0), "zb", swap)
    passed = lax.ppermute(fetched, "core", swap)

    slab = lax.optimization_barrier((fetched, near_own))[1]
    near_other = lax.ppermute(slab, "zb", swap)
    arrived = arrived.reshape(2 * ctx_count, part, padded)
    arrived, q_own, q_other = lax.optimization_barrier((arrived, q_own, q_other))
    for_partner, keys = attend_far(places, own_list, place, q_own, q_other, arrived, value_proj, fetched, passed)
    there = lax.ppermute(for_partner, "zb", swap)
    here = attend_near(own_list, place, q_own, q_other, keys, value_proj, fetched, passed, part)
    here, near_other = lax.optimization_barrier((here, near_other))
    far_other = lax.ppermute(near_other, "core", swap)
    gathered = lax.all_gather(merge(place, here, there, heads), ("x", "y"), axis=0, tiled=False)
    partial = project(place, gathered, near_own, near_other, far_own, far_other)
    partial = partial.reshape(-1, *partial.shape[2:])
    sent = lax.all_to_all(partial, ("core", "zq", "zb"), split_axis=0, concat_axis=0, tiled=True)
    return add_parts(sent.reshape(2, -1, PAIR, *sent.shape[1:]), columns).T


def solution(mesh):
    shape = (4, 4, 2, mesh.shape["head"] // PAIR, PAIR)
    fine = Mesh(mesh.devices.reshape(shape), ("x", "y", "core", "zq", "zb"))
    ctx, head = ("x", "y", "core"), ("zq", "zb")
    in_specs = (
        P(ctx, head, None),
        P(ctx, None),
        P(),
        P(head, None, None),
        P(head, ctx),
    )
    return jax.shard_map(on_device, mesh=fine, in_specs=in_specs, out_specs=P(head, ctx), check_vma=False)
```

```python
import functools
import math

import jax
import jax.numpy as jnp
from jax import lax
from jax.experimental import pallas as pl
from jax.experimental.pallas import tpu as pltpu
from jax.sharding import Mesh
from jax.sharding import PartitionSpec as P

NEG = -1e30
SCALE = 1.0 / 192.0**0.5
LOG2E = math.log2(math.e)
F32, BF16, S16 = jnp.float32, jnp.bfloat16, jnp.int16
LANES = 128
PAIR = 2
LIMIT = 24 * 1024 * 1024
WHOLE = 60 * 1024 * 1024
SMEM = pl.BlockSpec(memory_space=pltpu.SMEM)
VMEM = pl.BlockSpec(memory_space=pltpu.VMEM)
ANY = pl.BlockSpec(memory_space=pl.ANY)
HBM = pl.BlockSpec(memory_space=pltpu.HBM)
PARAMS = pltpu.CompilerParams(vmem_limit_bytes=LIMIT)


def row_code(peak):
    return jnp.ceil(jnp.log2(jnp.maximum(peak, 1e-30)) * 256.0)


def to_int(x, code):
    y = jnp.round(x * (jnp.exp2(code * (-1.0 / 256.0)) * 32767.0))
    return jnp.clip(y, -32767.0, 32767.0)


def scale_of(code):
    return jnp.exp2(code * (1.0 / 256.0)) * (1.0 / 32767.0)


def as_s16(x):
    return x.astype(jnp.int32).astype(S16)


def as_f32(x):
    return x.astype(jnp.int32).astype(F32)


def row_peak(x):
    return jnp.max(jnp.abs(x), axis=-1, keepdims=True)


def lane_ids(shape):
    return lax.broadcasted_iota(jnp.int32, shape, len(shape) - 1)


def dot_nt(a, b):
    return lax.dot_general(a, b, (((1,), (1,)), ((), ())), preferred_element_type=F32)


def dot_nn(a, b):
    return jnp.dot(a, b, preferred_element_type=F32)


def halves(x):
    high = x.astype(BF16)
    return high, (x - high.astype(F32)).astype(BF16)


def cost(flops, nbytes, exps=0):
    return pl.CostEstimate(flops=flops, bytes_accessed=nbytes, transcendentals=exps)


def parcel_kernel(owner, member, selected, latent_t, out, lists, stage, wide, coded, ids_v, ids, in_sems, id_sems, sems):
    width, total = latent_t.shape
    blocks, part, padded = coded.shape
    block = total // blocks
    groups = total // LANES
    fetch = pltpu.make_async_copy(selected, lists, id_sems.at[0])
    fetch.start()
    loads = []
    for n in range(groups):
        columns = pl.ds(n * LANES, LANES)
        load = pltpu.make_async_copy(latent_t.at[:, columns], stage.at[:, columns], in_sems.at[n])
        load.start()
        loads.append(load)
    fetch.wait()
    offset = lists[...] - owner[0] * blocks
    mine = (offset >= 0) & (offset < blocks)
    first = jnp.min(jnp.where(mine, offset, blocks), axis=1, keepdims=True)
    last = jnp.max(jnp.where(mine, offset, -1), axis=1, keepdims=True)
    ids_v[...] = jnp.where(lane_ids(ids_v.shape) == 0, first, last)
    move = pltpu.make_async_copy(ids_v, ids, id_sems.at[1])
    move.start()
    lanes = lane_ids((part, padded))
    for n in range(groups):
        loads[n].wait()
        wide[:, :width] = stage[:, n * LANES : (n + 1) * LANES].T
        for m in range(LANES // block):
            at = pl.multiple_of(m * block + member[0] * part, part)
            x = jnp.where(lanes < width, wide[pl.ds(at, part), :], 0.0)
            code = row_code(row_peak(x))
            full = jnp.where(lanes < width, to_int(x, code), code)
            coded[n * (LANES // block) + m] = as_s16(full)
    move.wait()
    copies = []
    for d in range(out.shape[0]):
        low, high = ids[d, 0], ids[d, 1]
        for s, (block_id, filled) in enumerate(((low, low <= high), (high, low < high))):
            copy = pltpu.make_async_copy(coded.at[jnp.clip(block_id, 0, blocks - 1)], out.at[d, s], sems.at[2 * d + s])
            pl.when(filled)(copy.start)
            copies.append((filled, copy))
    for filled, copy in copies:
        pl.when(filled)(copy.wait)


def make_parcels(owner, member, selected, latent_t, blocks, part, padded):
    receivers = selected.shape[0]
    width, total = latent_t.shape
    return pl.pallas_call(
        parcel_kernel,
        out_shape=jax.ShapeDtypeStruct((receivers, 2, part, padded), S16),
        in_specs=[SMEM, SMEM, HBM, HBM],
        out_specs=HBM,
        scratch_shapes=[
            pltpu.VMEM(selected.shape, jnp.int32),
            pltpu.VMEM((width, total), F32),
            pltpu.VMEM((LANES, padded), F32),
            pltpu.VMEM((blocks, part, padded), S16),
            pltpu.VMEM((receivers, LANES), jnp.int32),
            pltpu.SMEM((receivers, LANES), jnp.int32),
            pltpu.SemaphoreType.DMA((total // LANES,)),
            pltpu.SemaphoreType.DMA((2,)),
            pltpu.SemaphoreType.DMA((2 * receivers,)),
        ],
        compiler_params=pltpu.CompilerParams(vmem_limit_bytes=WHOLE),
        cost_estimate=cost(10**7, 4 * 10**6),
        name="parcels",
    )(owner, member, selected, latent_t)


def pack_kernel(q, out, wide):
    width = q.shape[-1]
    wide[:, :width] = q[...]
    lanes = lane_ids(wide.shape)
    x = jnp.where(lanes < width, wide[...], 0.0)
    code = row_code(row_peak(x))
    out[...] = as_s16(jnp.where(lanes < width, to_int(x, code), code))


def pack_queries(q, padded):
    rows = q.shape[0]
    return pl.pallas_call(
        pack_kernel,
        out_shape=jax.ShapeDtypeStruct((rows, padded), S16),
        in_specs=[VMEM],
        out_specs=VMEM,
        scratch_shapes=[pltpu.VMEM((rows, padded), F32)],
        compiler_params=PARAMS,
        cost_estimate=cost(10**7, 2 * 10**6),
        name="pack_queries",
    )(q)


def load_queries(place, half, own, other, q_s, heads):
    rows, padded = own.shape
    block = rows // heads
    part = block // PAIR
    some = heads // 2
    lat = padded - LANES
    core, member = place[0], place[1]
    begin = (member if half == 1 else 1 - member) * part
    rope = lane_ids((part, LANES)) < LANES // 2
    for n in range(PAIR * heads):
        head = n
        if n >= heads:
            head = ((n - heads) // some + core) % 2 * some + n % some
        at = pl.multiple_of(head * block + begin, part)
        wide = as_f32((own if n < heads else other)[pl.ds(at, part), :])
        wide = wide * (scale_of(wide[:, lat:])[:, LANES - 1 :] * (SCALE * LOG2E))
        span = slice(n * part, (n + 1) * part)
        high, low = halves(wide[:, :lat])
        q_s[span, :lat] = high
        q_s[span, lat : 2 * lat] = low
        high, low = halves(jnp.where(rope, wide[:, lat:], 0.0))
        both = high.astype(F32) + pltpu.roll(low.astype(F32), LANES // 2, 1)
        q_s[span, 2 * lat : 2 * lat + LANES] = both.astype(BF16)
        q_s[span, 2 * lat + LANES :] = high


def fetch_keys(places, arrived, slots, sems):
    copies = []
    for i in range(places.shape[0]):
        copy = pltpu.make_async_copy(arrived.at[places[i]], slots.at[i], sems.at[i])
        copy.start()
        copies.append(copy)
    return copies


def split_keys(copies, slots, keys_s):
    count, part, padded = slots.shape
    lat = padded - LANES
    step = 8
    rope = lane_ids((step * part, LANES)) < LANES // 2
    for c in range(count // step):
        for i in range(c * step, (c + 1) * step):
            copies[i].wait()
        wide = as_f32(slots[c * step : (c + 1) * step].reshape(step * part, padded))
        wide = wide * scale_of(wide[:, lat:])[:, LANES - 1 :]
        span = slice(c * step * part, (c + 1) * step * part)
        high, low = halves(wide[:, :lat])
        keys_s[span, :lat] = high
        keys_s[span, lat : 2 * lat] = low
        tail = jnp.where(rope, wide[:, lat:], 0.0)
        keys_s[span, 2 * lat : 2 * lat + LANES] = (tail + pltpu.roll(tail, LANES // 2, 1)).astype(BF16)
        keys_s[span, 2 * lat + LANES :] = halves(tail)[1]


def attend_rows(block_ids, place, half, q, keys_s, vp_own, fetched, passed, out):
    heads, lat, vdim = vp_own.shape
    count = block_ids.shape[0]
    part = out.shape[0]
    some = fetched.shape[0]
    keys = keys_s.shape[0]
    lane = lane_ids((1, keys))
    room = jnp.zeros((1, keys), jnp.int32)
    for i in range(count):
        room = jnp.where(lane // part == i, (place[2] - block_ids[i]) * (PAIR * part), room)
    if half == 0:
        room = room + (1 - 2 * place[1]) * part
    room = room - lane % part
    spot = lax.broadcasted_iota(jnp.int32, (q.shape[0], 1), 0) % part
    s = (
        dot_nt(q[:, :lat], keys_s[:, :lat])
        + dot_nt(q[:, lat : 2 * lat], keys_s[:, :lat])
        + dot_nt(q[:, :lat], keys_s[:, lat : 2 * lat])
        + dot_nt(q[:, 2 * lat :], keys_s[:, 2 * lat :])
    )
    s = jnp.where(room + spot >= 0, s, NEG)
    peak = jnp.max(s, axis=-1, keepdims=True)
    p = jnp.exp2(s - peak)
    norm = jnp.sum(p, axis=-1, keepdims=True)
    high, low = halves(p)
    mixed = dot_nn(high, keys_s[:, :lat]) + dot_nn(high, keys_s[:, lat : 2 * lat]) + dot_nn(low, keys_s[:, :lat])
    high, low = halves(mixed / norm)
    stat = (peak + jnp.log2(norm)) * 2.0
    coarse = jnp.floor(stat)
    fine = (stat - coarse) * 32767.0
    results = []
    for n in range(PAIR * heads):
        rows = slice(n * part, (n + 1) * part)
        maps = vp_own[n] if n < heads else (fetched[n - heads] if n < heads + some else passed[n - heads - some])
        both = dot_nn(jnp.concatenate([high[rows], low[rows]], axis=0), maps)
        results.append(both[:part] + both[part:])
    head_out = jnp.concatenate(results, axis=-1)
    code = row_code(row_peak(head_out))
    inner = head_out.shape[-1]
    coded = as_s16(to_int(head_out, code))
    half = inner // PAIR
    width = some * vdim
    out[:, :half] = coded[:, :half]
    for n, turn in enumerate((place[0], 1 - place[0])):
        at = pl.multiple_of(half + turn * width, width)
        out[:, pl.ds(at, width)] = coded[:, half + n * width : half + (n + 1) * width]
    lane = lane_ids((part, LANES))
    tail = code
    for n in range(PAIR * heads):
        rows = slice(n * part, (n + 1) * part)
        at = n
        if n >= heads:
            turn = place[0] if n < heads + some else 1 - place[0]
            at = heads + turn * some + n % some
        tail = jnp.where(lane == at, coarse[rows], tail)
        tail = jnp.where(lane == at + PAIR * heads, fine[rows], tail)
    out[:, inner:] = as_s16(tail)


def far_kernel(
    places, block_ids, place, own, other, arrived, vp_own, fetched, passed, out, keys_s, slots, q_s, sems
):
    copies = fetch_keys(places, arrived, slots, sems)
    load_queries(place, 0, own, other, q_s, vp_own.shape[0])
    split_keys(copies, slots, keys_s)
    attend_rows(block_ids, place, 0, q_s, keys_s, vp_own, fetched, passed, out)


def near_kernel(block_ids, place, own, other, keys_s, vp_own, fetched, passed, out, q_s):
    load_queries(place, 1, own, other, q_s, vp_own.shape[0])
    attend_rows(block_ids, place, 1, q_s, keys_s, vp_own, fetched, passed, out)


def attend_far(places, block_ids, place, own, other, arrived, vp_own, fetched, passed):
    count = places.shape[0]
    _, part, padded = arrived.shape
    heads, _, vdim = vp_own.shape
    return pl.pallas_call(
        far_kernel,
        out_shape=(
            jax.ShapeDtypeStruct((part, PAIR * heads * vdim + LANES), S16),
            jax.ShapeDtypeStruct((count * part, 2 * padded), BF16),
        ),
        in_specs=[SMEM, SMEM, SMEM, VMEM, VMEM, HBM, VMEM, VMEM, VMEM],
        out_specs=(VMEM, VMEM),
        scratch_shapes=[
            pltpu.VMEM((count, part, padded), S16),
            pltpu.VMEM((own.shape[0], 2 * padded), BF16),
            pltpu.SemaphoreType.DMA((count,)),
        ],
        compiler_params=PARAMS,
        cost_estimate=cost(4 * 10**9, 6 * 10**6, 10**6),
        name="attend_far",
    )(places, block_ids, place, own, other, arrived, vp_own, fetched, passed)


def attend_near(block_ids, place, own, other, keys, vp_own, fetched, passed, part):
    heads, _, vdim = vp_own.shape
    return pl.pallas_call(
        near_kernel,
        out_shape=jax.ShapeDtypeStruct((part, PAIR * heads * vdim + LANES), S16),
        in_specs=[SMEM, SMEM, VMEM, VMEM, VMEM, VMEM, VMEM, VMEM],
        out_specs=VMEM,
        scratch_shapes=[pltpu.VMEM((own.shape[0], 2 * own.shape[1]), BF16)],
        compiler_params=PARAMS,
        cost_estimate=cost(4 * 10**9, 6 * 10**6, 10**6),
        name="attend_near",
    )(block_ids, place, own, other, keys, vp_own, fetched, passed)


def merge_kernel(place, here, there, out, *, heads):
    rows, padded = here.shape
    inner = padded - LANES
    width = inner // PAIR
    vdim = width // heads
    tails = [as_f32(x[:, inner:]) for x in (here, there)]
    logs = [(x + pltpu.roll(x, LANES - PAIR * heads, 1) * (1.0 / 32767.0)) * 0.5 for x in tails]
    scales = [scale_of(x)[:, LANES - 1 :] for x in tails]
    merged = []
    for g in range(PAIR):
        a = logs[0] if g == 0 else pltpu.roll(logs[0], LANES - heads, 1)
        b = logs[1] if g == 1 else pltpu.roll(logs[1], LANES - heads, 1)
        top = jnp.maximum(a, b)
        a, b = jnp.exp2(a - top), jnp.exp2(b - top)
        total = a + b
        a, b = a / total * scales[0], b / total * scales[1]
        for h in range(heads):
            x = as_f32(here[:, g * width + h * vdim : g * width + (h + 1) * vdim]) * a[:, h : h + 1]
            y = as_f32(there[:, (1 - g) * width + h * vdim : (1 - g) * width + (h + 1) * vdim]) * b[:, h : h + 1]
            merged.append((x + y).astype(BF16).astype(F32))
    head_out = jnp.concatenate(merged, axis=-1)
    code = row_code(row_peak(head_out))
    coded = as_s16(to_int(head_out, code))
    for g, turn in enumerate((place[1], 1 - place[1])):
        out[:, pl.ds(pl.multiple_of(turn * width, width), width)] = coded[:, g * width : (g + 1) * width]
    out[:, inner:] = as_s16(jnp.broadcast_to(code, (rows, LANES)))


def merge(place, here, there, heads):
    return pl.pallas_call(
        functools.partial(merge_kernel, heads=heads),
        out_shape=jax.ShapeDtypeStruct(here.shape, S16),
        in_specs=[SMEM, VMEM, VMEM],
        out_specs=VMEM,
        compiler_params=PARAMS,
        cost_estimate=cost(10**6, 5 * 10**5),
        name="merge",
    )(place, here, there)


def project_kernel(place, rows_in, near_own, near_other, far_own, far_other, out, wide):
    chips, rows, padded = rows_in.shape
    inner = padded - LANES
    columns, depth = near_own.shape
    core = place[0]
    factor = scale_of(as_f32(rows_in[:, :, inner:]).reshape(chips * rows, LANES))[:, :1]
    sums = [None, None]
    for n, member in enumerate((place[1], 1 - place[1])):
        at = pl.multiple_of(member * depth, depth)
        a = as_f32(rows_in[:, :, pl.ds(at, depth)]).reshape(chips * rows, depth)
        a = (a * factor).astype(BF16)
        for k, weights in enumerate(((near_own, far_own), (near_other, far_other))[n]):
            term = dot_nt(a, weights[...])
            sums[k] = term if n == 0 else sums[k] + term
    spare = 2 * LANES - columns
    keep = LANES - spare
    groups = rows // 8
    for k, at in enumerate((core, 1 - core)):
        wide[:, :columns] = sums[k]
        out[at, :, :rows, :] = wide[:, :LANES].reshape(chips, rows, LANES).astype(BF16)
        rest = wide[:, LANES:].reshape(chips, groups, 8, LANES)
        last = rest[:, groups - 1].reshape(chips * 8, LANES)
        lanes = lane_ids(last.shape)
        packed = []
        for g in range(groups - 1):
            moved = pltpu.roll(last, (keep - spare * g) % LANES, 1)
            packed.append(jnp.where(lanes < keep, rest[:, g].reshape(chips * 8, LANES), moved))
        packed = jnp.concatenate([x.reshape(chips, 8, LANES) for x in packed], axis=1)
        out[at, :, rows:, :] = packed.astype(BF16)


def project(place, rows_in, near_own, near_other, far_own, far_other):
    chips, rows, _ = rows_in.shape
    return pl.pallas_call(
        project_kernel,
        out_shape=jax.ShapeDtypeStruct((2, chips, rows * near_own.shape[0] // LANES, LANES), BF16),
        in_specs=[SMEM] + [VMEM] * 5,
        out_specs=VMEM,
        scratch_shapes=[pltpu.VMEM((chips * rows, 2 * LANES), F32)],
        compiler_params=PARAMS,
        cost_estimate=cost(10**9, 7 * 10**6),
        name="project",
    )(place, rows_in, near_own, near_other, far_own, far_other)


def add_kernel(parts, out):
    cores, outer, groups, packed, _ = parts.shape
    columns, total = out.shape
    rows = total // (cores * groups)
    spare = 2 * LANES - columns
    keep = LANES - spare
    lanes = lane_ids((8, LANES))
    left, right = [], []
    for k in range(cores):
        for g in range(groups):
            full = parts[k, 0, g].astype(F32)
            for z in range(1, outer):
                full = full + parts[k, z, g].astype(F32)
            left.append(full[:rows])
            pieces = [full[rows + 8 * n : rows + 8 * (n + 1)] for n in range(rows // 8 - 1)]
            last = jnp.zeros((8, LANES), F32)
            for n, piece in enumerate(pieces):
                moved = pltpu.roll(piece, (spare * n - keep) % LANES, 1)
                last = jnp.where((lanes >= spare * n) & (lanes < spare * (n + 1)), moved, last)
            right.extend(pieces + [last])
    out[:LANES, :] = jnp.concatenate(left, axis=0).T.astype(BF16)
    out[LANES:, :] = jnp.concatenate(right, axis=0).T[: columns - LANES].astype(BF16)


def add_parts(parts, columns):
    cores, _, groups, packed, _ = parts.shape
    rows = packed * LANES // columns
    return pl.pallas_call(
        add_kernel,
        out_shape=jax.ShapeDtypeStruct((columns, cores * groups * rows), BF16),
        in_specs=[VMEM],
        out_specs=VMEM,
        name="add_parts",
    )(parts)


def on_device(queries, latent, selected, value_proj, out_proj):
    plane = ("x", "y", "core")
    ctx_count = lax.axis_size(plane)
    ctx_index = lax.axis_index(plane)
    core = lax.axis_index("core").astype(jnp.int32)
    member = lax.axis_index("zb").astype(jnp.int32)
    block, heads, width = queries.shape
    per_owner = latent.shape[0] // block
    key_blocks = per_owner * ctx_count
    padded = -(-width // LANES) * LANES
    columns = out_proj.shape[1]
    part = block // PAIR
    swap = [(0, 1), (1, 0)]

    parcels = make_parcels(ctx_index[None].astype(jnp.int32), member[None], selected, latent.T, per_owner, part, padded)
    parcels, queries, value_near = lax.optimization_barrier((parcels, queries, value_proj))
    arrived = lax.all_to_all(parcels, plane, split_axis=0, concat_axis=0, tiled=True)

    q = jnp.transpose(queries, (1, 0, 2)).reshape(heads * block, width)
    near_own = out_proj.T
    q_own = pack_queries(q, padded)
    q_other = lax.ppermute(q_own, "zb", swap)
    near_own = lax.optimization_barrier((q_own, near_own))[1]
    far_own = lax.ppermute(near_own, "core", swap)
    place = jnp.stack([core, member, key_blocks - ctx_count + ctx_index]).astype(jnp.int32)

    fetched = lax.ppermute(lax.dynamic_slice_in_dim(value_near, core * (heads // 2), heads // 2, 0), "zb", swap)
    passed = lax.ppermute(fetched, "core", swap)
    listed = lax.optimization_barrier((fetched, selected))[1]
    own_list = lax.dynamic_slice_in_dim(listed, ctx_index, 1, 0)[0]
    owner = own_list // per_owner
    second = jnp.any((owner[None, :] == owner[:, None]) & (own_list[None, :] < own_list[:, None]), axis=1)
    places = owner * 2 + second.astype(jnp.int32)

    slab = lax.optimization_barrier((fetched, near_own))[1]
    near_other = lax.ppermute(slab, "zb", swap)
    arrived = arrived.reshape(2 * ctx_count, part, padded)
    arrived, q_own, q_other = lax.optimization_barrier((arrived, q_own, q_other))
    for_partner, keys = attend_far(places, own_list, place, q_own, q_other, arrived, value_proj, fetched, passed)
    there = lax.ppermute(for_partner, "zb", swap)
    here = attend_near(own_list, place, q_own, q_other, keys, value_proj, fetched, passed, part)
    here, near_other = lax.optimization_barrier((here, near_other))
    far_other = lax.ppermute(near_other, "core", swap)
    gathered = lax.all_gather(merge(place, here, there, heads), ("x", "y"), axis=0, tiled=False)
    partial = project(place, gathered, near_own, near_other, far_own, far_other)
    partial = partial.reshape(-1, *partial.shape[2:])
    sent = lax.all_to_all(partial, ("core", "zq", "zb"), split_axis=0, concat_axis=0, tiled=True)
    return add_parts(sent.reshape(2, -1, PAIR, *sent.shape[1:]), columns).T


def solution(mesh):
    shape = (4, 4, 2, mesh.shape["head"] // PAIR, PAIR)
    fine = Mesh(mesh.devices.reshape(shape), ("x", "y", "core", "zq", "zb"))
    ctx, head = ("x", "y", "core"), ("zq", "zb")
    in_specs = (
        P(ctx, head, None),
        P(ctx, None),
        P(),
        P(head, None, None),
        P(head, ctx),
    )
    return jax.shard_map(on_device, mesh=fine, in_specs=in_specs, out_specs=P(head, ctx), check_vma=False)
```

```python
import functools
import math

import jax
import jax.numpy as jnp
from jax import lax
from jax.experimental import pallas as pl
from jax.experimental.pallas import tpu as pltpu
from jax.sharding import Mesh
from jax.sharding import PartitionSpec as P

NEG = -1e30
SCALE = 1.0 / 192.0**0.5
LOG2E = math.log2(math.e)
F32, BF16, S16 = jnp.float32, jnp.bfloat16, jnp.int16
LANES = 128
PAIR = 2
LIMIT = 32 * 1024 * 1024
WHOLE = 60 * 1024 * 1024
SMEM = pl.BlockSpec(memory_space=pltpu.SMEM)
VMEM = pl.BlockSpec(memory_space=pltpu.VMEM)
ANY = pl.BlockSpec(memory_space=pl.ANY)
HBM = pl.BlockSpec(memory_space=pltpu.HBM)
PARAMS = pltpu.CompilerParams(vmem_limit_bytes=LIMIT)


def row_code(peak):
    return jnp.ceil(jnp.log2(jnp.maximum(peak, 1e-30)) * 256.0)


def to_int(x, code):
    y = jnp.round(x * (jnp.exp2(code * (-1.0 / 256.0)) * 32767.0))
    return jnp.clip(y, -32767.0, 32767.0)


def scale_of(code):
    return jnp.exp2(code * (1.0 / 256.0)) * (1.0 / 32767.0)


def as_s16(x):
    return x.astype(jnp.int32).astype(S16)


def as_f32(x):
    return x.astype(jnp.int32).astype(F32)


def row_peak(x):
    return jnp.max(jnp.abs(x), axis=-1, keepdims=True)


def lane_ids(shape):
    return lax.broadcasted_iota(jnp.int32, shape, len(shape) - 1)


def dot_nt(a, b):
    return lax.dot_general(a, b, (((1,), (1,)), ((), ())), preferred_element_type=F32)


def dot_nn(a, b):
    return jnp.dot(a, b, preferred_element_type=F32)


def halves(x):
    high = x.astype(BF16)
    return high, (x - high.astype(F32)).astype(BF16)


def cost(flops, nbytes, exps=0):
    return pl.CostEstimate(flops=flops, bytes_accessed=nbytes, transcendentals=exps)


def place_of(ctx, count, columns):
    rest = count // columns
    return ctx % rest * columns + ctx // rest


def parcel_kernel(
    owner, member, selected, latent_t, out, lists, stage, wide, coded, ids_v, ids, in_sems, id_sems, sems, *, columns
):
    width, total = latent_t.shape
    blocks, part, padded = coded.shape
    block = total // blocks
    groups = total // LANES
    fetch = pltpu.make_async_copy(selected, lists, id_sems.at[0])
    fetch.start()
    loads = []
    for n in range(groups):
        span = pl.ds(n * LANES, LANES)
        load = pltpu.make_async_copy(latent_t.at[:, span], stage.at[:, span], in_sems.at[n])
        load.start()
        loads.append(load)
    fetch.wait()
    offset = lists[...] - owner[0] * blocks
    mine = (offset >= 0) & (offset < blocks)
    first = jnp.min(jnp.where(mine, offset, blocks), axis=1, keepdims=True)
    last = jnp.max(jnp.where(mine, offset, -1), axis=1, keepdims=True)
    ids_v[...] = jnp.where(lane_ids(ids_v.shape) == 0, first, last)
    move = pltpu.make_async_copy(ids_v, ids, id_sems.at[1])
    move.start()
    lanes = lane_ids((part, padded))
    for n in range(groups):
        loads[n].wait()
        wide[:, :width] = stage[:, n * LANES : (n + 1) * LANES].T
        for m in range(LANES // block):
            at = pl.multiple_of(m * block + member[0] * part, part)
            x = jnp.where(lanes < width, wide[pl.ds(at, part), :], 0.0)
            code = row_code(row_peak(x))
            full = jnp.where(lanes < width, to_int(x, code), code)
            coded[n * (LANES // block) + m] = as_s16(full)
    move.wait()
    copies = []
    for d in range(out.shape[0]):
        low, high = ids[d, 0], ids[d, 1]
        for s, (block_id, filled) in enumerate(((low, low <= high), (high, low < high))):
            source = coded.at[jnp.clip(block_id, 0, blocks - 1)]
            copy = pltpu.make_async_copy(source, out.at[place_of(d, out.shape[0], columns), s], sems.at[2 * d + s])
            pl.when(filled)(copy.start)
            copies.append((filled, copy))
    for filled, copy in copies:
        pl.when(filled)(copy.wait)


def make_parcels(owner, member, selected, latent_t, blocks, part, padded, columns):
    receivers = selected.shape[0]
    width, total = latent_t.shape
    return pl.pallas_call(
        functools.partial(parcel_kernel, columns=columns),
        out_shape=jax.ShapeDtypeStruct((receivers, 2, part, padded), S16),
        in_specs=[SMEM, SMEM, HBM, HBM],
        out_specs=HBM,
        scratch_shapes=[
            pltpu.VMEM(selected.shape, jnp.int32),
            pltpu.VMEM((width, total), F32),
            pltpu.VMEM((LANES, padded), F32),
            pltpu.VMEM((blocks, part, padded), S16),
            pltpu.VMEM((receivers, LANES), jnp.int32),
            pltpu.SMEM((receivers, LANES), jnp.int32),
            pltpu.SemaphoreType.DMA((total // LANES,)),
            pltpu.SemaphoreType.DMA((2,)),
            pltpu.SemaphoreType.DMA((2 * receivers,)),
        ],
        compiler_params=pltpu.CompilerParams(vmem_limit_bytes=WHOLE),
        cost_estimate=cost(10**7, 4 * 10**6),
        name="parcels",
    )(owner, member, selected, latent_t)


def pack_kernel(q, out):
    rows, width = q.shape
    main = width // LANES
    code = row_code(row_peak(jnp.max(jnp.abs(q[...]), axis=0, keepdims=True)))
    for t in range(main):
        out[t * rows : (t + 1) * rows, :] = as_s16(to_int(q[:, t * LANES : (t + 1) * LANES], code))
    rest = to_int(q[:, main * LANES :], code)
    both = jnp.concatenate([rest[: rows // 2], rest[rows // 2 :]], axis=-1)
    out[main * rows : main * rows + rows // 2, :] = as_s16(both)
    out[main * rows + rows // 2 :, :] = as_s16(jnp.broadcast_to(code, (16, LANES)))


def pack_queries(q):
    rows, width = q.shape
    return pl.pallas_call(
        pack_kernel,
        out_shape=jax.ShapeDtypeStruct((rows * width // LANES + 16, LANES), S16),
        in_specs=[VMEM],
        out_specs=VMEM,
        compiler_params=PARAMS,
        cost_estimate=cost(10**7, 2 * 10**6),
        name="pack_queries",
    )(q)


def load_queries(place, half, own, other, q_s):
    some = q_s.shape[0] // PAIR
    lat = (q_s.shape[1] - 2 * LANES) // 2
    rows = PAIR * some
    turn = place[1] if half == 1 else 1 - place[1]
    lanes = lane_ids((some, LANES))
    for n, q in enumerate((own, other)):
        end = q.shape[0] - 16
        factor = scale_of(as_f32(q[end:, :]))[:1, :1] * (SCALE * LOG2E)
        span = slice(n * some, (n + 1) * some)
        for t in range(lat // LANES):
            at = pl.multiple_of(t * rows + turn * some, some)
            high, low = halves(as_f32(q[pl.ds(at, some), :]) * factor)
            q_s[span, t * LANES : (t + 1) * LANES] = high
            q_s[span, lat + t * LANES : lat + (t + 1) * LANES] = low
        rest = as_f32(q[end - some : end, :]) * factor
        rest = jnp.where(turn == 0, rest, pltpu.roll(rest, LANES // 2, 1))
        high, low = halves(jnp.where(lanes < LANES // 2, rest, 0.0))
        both = high.astype(F32) + pltpu.roll(low.astype(F32), LANES // 2, 1)
        q_s[span, 2 * lat : 2 * lat + LANES] = both.astype(BF16)
        q_s[span, 2 * lat + LANES :] = high


def half_kernel(core, values, half, sem):
    some = half.shape[0]
    copy = pltpu.make_async_copy(values.at[pl.ds(core[0] * some, some)], half, sem)
    copy.start()
    copy.wait()


def half_values(core, values):
    heads, lat, vdim = values.shape
    return pl.pallas_call(
        half_kernel,
        out_shape=jax.ShapeDtypeStruct((heads // 2, lat, vdim), BF16),
        in_specs=[SMEM, HBM],
        out_specs=VMEM,
        scratch_shapes=[pltpu.SemaphoreType.DMA],
        compiler_params=pltpu.CompilerParams(vmem_limit_bytes=WHOLE),
        cost_estimate=cost(10**4, 10**6),
        name="half_values",
    )(core, values)


def split_keys(places, arrived, keys_s):
    count = places.shape[0]
    _, part, padded = arrived.shape
    lat = padded - LANES
    rope = lane_ids((part, LANES)) < LANES // 2
    for i in range(count):
        wide = as_f32(arrived[places[i]])
        wide = wide * scale_of(wide[:, lat:])[:, LANES - 1 :]
        span = slice(i * part, (i + 1) * part)
        high, low = halves(wide[:, :lat])
        keys_s[span, :lat] = high
        keys_s[span, lat : 2 * lat] = low
        tail = jnp.where(rope, wide[:, lat:], 0.0)
        keys_s[span, 2 * lat : 2 * lat + LANES] = (tail + pltpu.roll(tail, LANES // 2, 1)).astype(BF16)
        keys_s[span, 2 * lat + LANES :] = halves(tail)[1]


def attend_rows(block_ids, place, half, q, keys_s, vp_own, fetched, passed, out, mixed_s, stat_s):
    heads, lat, vdim = vp_own.shape
    count = block_ids.shape[0]
    part = out.shape[0]
    some = fetched.shape[0]
    keys = keys_s.shape[0]
    lane = lane_ids((1, keys))
    room = jnp.zeros((1, keys), jnp.int32)
    for i in range(count):
        room = jnp.where(lane // part == i, (place[2] - block_ids[i]) * (PAIR * part), room)
    if half == 0:
        room = room + (1 - 2 * place[1]) * part
    room = room - lane % part
    spot = lax.broadcasted_iota(jnp.int32, (q.shape[0], 1), 0) // heads % part
    s = (
        dot_nt(q[:, :lat], keys_s[:, :lat])
        + dot_nt(q[:, lat : 2 * lat], keys_s[:, :lat])
        + dot_nt(q[:, :lat], keys_s[:, lat : 2 * lat])
        + dot_nt(q[:, 2 * lat :], keys_s[:, 2 * lat :])
    )
    s = jnp.where(room + spot >= 0, s, NEG)
    peak = jnp.max(s, axis=-1, keepdims=True)
    p = jnp.exp2(s - peak)
    norm = jnp.sum(p, axis=-1, keepdims=True)
    high, low = halves(p)
    mixed = dot_nn(high, keys_s[:, :lat]) + dot_nn(high, keys_s[:, lat : 2 * lat]) + dot_nn(low, keys_s[:, :lat])
    mixed = mixed / norm
    for t in range(lat // LANES):
        mixed_s[t] = mixed[:, t * LANES : (t + 1) * LANES]
    stat_s[...] = jnp.broadcast_to((peak + jnp.log2(norm)) * 2.0, stat_s.shape)
    results, stats = [], []
    for n in range(PAIR * heads):
        head = n if n < heads else heads * part + ((n - heads) // some + place[0]) % 2 * some + n % some
        rows = pl.ds(head, part, stride=heads)
        high, low = halves(jnp.concatenate([mixed_s[t, rows, :] for t in range(lat // LANES)], axis=-1))
        maps = vp_own[n] if n < heads else (fetched[n - heads] if n < heads + some else passed[n - heads - some])
        both = dot_nn(jnp.concatenate([high, low], axis=0), maps)
        results.append(both[:part] + both[part:])
        stats.append(stat_s[rows, :])
    head_out = jnp.concatenate(results, axis=-1)
    code = row_code(row_peak(head_out))
    inner = head_out.shape[-1]
    coded = as_s16(to_int(head_out, code))
    half = inner // PAIR
    width = some * vdim
    out[:, :half] = coded[:, :half]
    for n, turn in enumerate((place[0], 1 - place[0])):
        at = pl.multiple_of(half + turn * width, width)
        out[:, pl.ds(at, width)] = coded[:, half + n * width : half + (n + 1) * width]
    lane = lane_ids((part, LANES))
    tail = code
    for n in range(PAIR * heads):
        at = n
        if n >= heads:
            turn = place[0] if n < heads + some else 1 - place[0]
            at = heads + turn * some + n % some
        coarse = jnp.floor(stats[n])
        tail = jnp.where(lane == at, coarse, tail)
        tail = jnp.where(lane == at + PAIR * heads, (stats[n] - coarse) * 32767.0, tail)
    out[:, inner:] = as_s16(tail)


def far_kernel(
    places, block_ids, place, own, other, arrived, vp_own, fetched, passed, out, keys_s, q_s, mixed_s, stat_s
):
    load_queries(place, 0, own, other, q_s)
    split_keys(places, arrived, keys_s)
    attend_rows(block_ids, place, 0, q_s, keys_s, vp_own, fetched, passed, out, mixed_s, stat_s)


def near_kernel(block_ids, place, own, other, keys_s, vp_own, fetched, passed, out, q_s, mixed_s, stat_s):
    load_queries(place, 1, own, other, q_s)
    attend_rows(block_ids, place, 1, q_s, keys_s, vp_own, fetched, passed, out, mixed_s, stat_s)


def attend_far(places, block_ids, place, own, other, arrived, vp_own, fetched, passed):
    count = places.shape[0]
    _, part, padded = arrived.shape
    heads, lat, vdim = vp_own.shape
    rows = PAIR * heads * part
    return pl.pallas_call(
        far_kernel,
        out_shape=(
            jax.ShapeDtypeStruct((part, PAIR * heads * vdim + LANES), S16),
            jax.ShapeDtypeStruct((count * part, 2 * padded), BF16),
        ),
        in_specs=[SMEM, SMEM, SMEM] + [VMEM] * 6,
        out_specs=(VMEM, VMEM),
        scratch_shapes=[
            pltpu.VMEM((rows, 2 * padded), BF16),
            pltpu.VMEM((lat // LANES, rows, LANES), F32),
            pltpu.VMEM((rows, LANES), F32),
        ],
        compiler_params=PARAMS,
        cost_estimate=cost(4 * 10**9, 6 * 10**6, 10**6),
        name="attend_far",
    )(places, block_ids, place, own, other, arrived, vp_own, fetched, passed)


def attend_near(block_ids, place, own, other, keys, vp_own, fetched, passed, part):
    heads, lat, vdim = vp_own.shape
    rows = PAIR * heads * part
    return pl.pallas_call(
        near_kernel,
        out_shape=jax.ShapeDtypeStruct((part, PAIR * heads * vdim + LANES), S16),
        in_specs=[SMEM, SMEM, VMEM, VMEM, VMEM, VMEM, VMEM, VMEM],
        out_specs=VMEM,
        scratch_shapes=[
            pltpu.VMEM((rows, keys.shape[1]), BF16),
            pltpu.VMEM((lat // LANES, rows, LANES), F32),
            pltpu.VMEM((rows, LANES), F32),
        ],
        compiler_params=PARAMS,
        cost_estimate=cost(4 * 10**9, 6 * 10**6, 10**6),
        name="attend_near",
    )(block_ids, place, own, other, keys, vp_own, fetched, passed)


def merge_kernel(place, here, there, out, *, heads):
    rows, padded = here.shape
    inner = padded - LANES
    width = inner // PAIR
    vdim = width // heads
    tails = [as_f32(x[:, inner:]) for x in (here, there)]
    logs = [(x + pltpu.roll(x, LANES - PAIR * heads, 1) * (1.0 / 32767.0)) * 0.5 for x in tails]
    scales = [scale_of(x)[:, LANES - 1 :] for x in tails]
    merged = []
    for g in range(PAIR):
        a = logs[0] if g == 0 else pltpu.roll(logs[0], LANES - heads, 1)
        b = logs[1] if g == 1 else pltpu.roll(logs[1], LANES - heads, 1)
        top = jnp.maximum(a, b)
        a, b = jnp.exp2(a - top), jnp.exp2(b - top)
        total = a + b
        a, b = a / total * scales[0], b / total * scales[1]
        for h in range(heads):
            x = as_f32(here[:, g * width + h * vdim : g * width + (h + 1) * vdim]) * a[:, h : h + 1]
            y = as_f32(there[:, (1 - g) * width + h * vdim : (1 - g) * width + (h + 1) * vdim]) * b[:, h : h + 1]
            merged.append((x + y).astype(BF16).astype(F32))
    head_out = jnp.concatenate(merged, axis=-1)
    code = row_code(row_peak(head_out))
    coded = as_s16(to_int(head_out, code))
    for g, turn in enumerate((place[1], 1 - place[1])):
        out[:, pl.ds(pl.multiple_of(turn * width, width), width)] = coded[:, g * width : (g + 1) * width]
    out[:, inner:] = as_s16(jnp.broadcast_to(code, (rows, LANES)))


def merge(place, here, there, heads):
    return pl.pallas_call(
        functools.partial(merge_kernel, heads=heads),
        out_shape=jax.ShapeDtypeStruct(here.shape, S16),
        in_specs=[SMEM, VMEM, VMEM],
        out_specs=VMEM,
        compiler_params=PARAMS,
        cost_estimate=cost(10**6, 5 * 10**5),
        name="merge",
    )(place, here, there)


def project_kernel(place, rows_in, near_own, near_other, far_own, far_other, out, wide):
    chips, rows, padded = rows_in.shape
    inner = padded - LANES
    columns, depth = near_own.shape
    core = place[0]
    factor = scale_of(as_f32(rows_in[:, :, inner:]).reshape(chips * rows, LANES))[:, :1]
    sums = [None, None]
    for n, member in enumerate((place[1], 1 - place[1])):
        at = pl.multiple_of(member * depth, depth)
        a = as_f32(rows_in[:, :, pl.ds(at, depth)]).reshape(chips * rows, depth)
        a = (a * factor).astype(BF16)
        for k, weights in enumerate(((near_own, far_own), (near_other, far_other))[n]):
            term = dot_nt(a, weights[...])
            sums[k] = term if n == 0 else sums[k] + term
    spare = 2 * LANES - columns
    keep = LANES - spare
    groups = rows // 8
    for k, at in enumerate((core, 1 - core)):
        wide[:, :columns] = sums[k]
        out[at, :, :rows, :] = wide[:, :LANES].reshape(chips, rows, LANES).astype(BF16)
        rest = wide[:, LANES:].reshape(chips, groups, 8, LANES)
        last = rest[:, groups - 1].reshape(chips * 8, LANES)
        lanes = lane_ids(last.shape)
        packed = []
        for g in range(groups - 1):
            moved = pltpu.roll(last, (keep - spare * g) % LANES, 1)
            packed.append(jnp.where(lanes < keep, rest[:, g].reshape(chips * 8, LANES), moved))
        packed = jnp.concatenate([x.reshape(chips, 8, LANES) for x in packed], axis=1)
        out[at, :, rows:, :] = packed.astype(BF16)


def project(place, rows_in, near_own, near_other, far_own, far_other):
    chips, rows, _ = rows_in.shape
    return pl.pallas_call(
        project_kernel,
        out_shape=jax.ShapeDtypeStruct((2, chips, rows * near_own.shape[0] // LANES, LANES), BF16),
        in_specs=[SMEM] + [VMEM] * 5,
        out_specs=VMEM,
        scratch_shapes=[pltpu.VMEM((chips * rows, 2 * LANES), F32)],
        compiler_params=PARAMS,
        cost_estimate=cost(10**9, 7 * 10**6),
        name="project",
    )(place, rows_in, near_own, near_other, far_own, far_other)


def add_kernel(parts, out):
    cores, outer, groups, packed, _ = parts.shape
    columns, total = out.shape
    rows = total // (cores * groups)
    spare = 2 * LANES - columns
    keep = LANES - spare
    lanes = lane_ids((8, LANES))
    left, right = [], []
    for k in range(cores):
        for g in range(groups):
            full = parts[k, 0, g].astype(F32)
            for z in range(1, outer):
                full = full + parts[k, z, g].astype(F32)
            left.append(full[:rows])
            pieces = [full[rows + 8 * n : rows + 8 * (n + 1)] for n in range(rows // 8 - 1)]
            last = jnp.zeros((8, LANES), F32)
            for n, piece in enumerate(pieces):
                moved = pltpu.roll(piece, (spare * n - keep) % LANES, 1)
                last = jnp.where((lanes >= spare * n) & (lanes < spare * (n + 1)), moved, last)
            right.extend(pieces + [last])
    out[:LANES, :] = jnp.concatenate(left, axis=0).T.astype(BF16)
    out[LANES:, :] = jnp.concatenate(right, axis=0).T[: columns - LANES].astype(BF16)


def add_parts(parts, columns):
    cores, _, groups, packed, _ = parts.shape
    rows = packed * LANES // columns
    return pl.pallas_call(
        add_kernel,
        out_shape=jax.ShapeDtypeStruct((columns, cores * groups * rows), BF16),
        in_specs=[VMEM],
        out_specs=VMEM,
        name="add_parts",
    )(parts)


def on_device(queries, latent, selected, value_proj, out_proj):
    plane = ("x", "y", "core")
    ctx_count = lax.axis_size(plane)
    ctx_index = lax.axis_index(plane)
    core = lax.axis_index("core").astype(jnp.int32)
    member = lax.axis_index("zb").astype(jnp.int32)
    block, heads, width = queries.shape
    per_owner = latent.shape[0] // block
    key_blocks = per_owner * ctx_count
    padded = -(-width // LANES) * LANES
    columns = out_proj.shape[1]
    part = block // PAIR
    swap = [(0, 1), (1, 0)]

    parcels = make_parcels(ctx_index[None].astype(jnp.int32), member[None], selected, latent.T, per_owner, part, padded, lax.axis_size("x"))
    parcels, queries, value_near = lax.optimization_barrier((parcels, queries, value_proj))
    arrived = lax.all_to_all(parcels, ("y", "core", "x"), split_axis=0, concat_axis=0, tiled=True)

    q = queries.reshape(block * heads, width)
    near_own = out_proj.T
    q_own = pack_queries(q)
    q_other = lax.ppermute(q_own, "zb", swap)
    near_own = lax.optimization_barrier((q_own, near_own))[1]
    far_own = lax.ppermute(near_own, "core", swap)
    place = jnp.stack([core, member, key_blocks - ctx_count + ctx_index]).astype(jnp.int32)

    fetched = lax.ppermute(half_values(core[None], value_near), "zb", swap)
    passed = lax.ppermute(fetched, "core", swap)
    listed = lax.optimization_barrier((fetched, selected))[1]
    own_list = lax.dynamic_slice_in_dim(listed, ctx_index, 1, 0)[0]
    owner = own_list // per_owner
    second = jnp.any((owner[None, :] == owner[:, None]) & (own_list[None, :] < own_list[:, None]), axis=1)
    places = place_of(owner, ctx_count, lax.axis_size("x")) * 2 + second.astype(jnp.int32)

    slab = lax.optimization_barrier((fetched, near_own))[1]
    near_other = lax.ppermute(slab, "zb", swap)
    arrived = arrived.reshape(2 * ctx_count, part, padded)
    arrived, q_own, q_other = lax.optimization_barrier((arrived, q_own, q_other))
    for_partner, keys = attend_far(places, own_list, place, q_own, q_other, arrived, value_proj, fetched, passed)
    there = lax.ppermute(for_partner, "zb", swap)
    here = attend_near(own_list, place, q_own, q_other, keys, value_proj, fetched, passed, part)
    here, near_other = lax.optimization_barrier((here, near_other))
    far_other = lax.ppermute(near_other, "core", swap)
    gathered = lax.all_gather(merge(place, here, there, heads), ("x", "y"), axis=0, tiled=False)
    partial = project(place, gathered, near_own, near_other, far_own, far_other)
    partial = partial.reshape(-1, *partial.shape[2:])
    sent = lax.all_to_all(partial, ("core", "zq", "zb"), split_axis=0, concat_axis=0, tiled=True)
    return add_parts(sent.reshape(2, -1, PAIR, *sent.shape[1:]), columns).T


def solution(mesh):
    shape = (4, 4, 2, mesh.shape["head"] // PAIR, PAIR)
    fine = Mesh(mesh.devices.reshape(shape), ("x", "y", "core", "zq", "zb"))
    ctx, head = ("x", "y", "core"), ("zq", "zb")
    in_specs = (
        P(ctx, head, None),
        P(ctx, None),
        P(),
        P(head, None, None),
        P(head, ctx),
    )
    return jax.shard_map(on_device, mesh=fine, in_specs=in_specs, out_specs=P(head, ctx), check_vma=False)
```

```python
import functools
import math

import jax
import jax.numpy as jnp
from jax import lax
from jax.experimental import pallas as pl
from jax.experimental.pallas import tpu as pltpu
from jax.sharding import Mesh
from jax.sharding import PartitionSpec as P

NEG = -1e30
SCALE = 1.0 / 192.0**0.5
LOG2E = math.log2(math.e)
F32, BF16, S16 = jnp.float32, jnp.bfloat16, jnp.int16
LANES = 128
PAIR = 2
LIMIT = 32 * 1024 * 1024
WHOLE = 60 * 1024 * 1024
SMEM = pl.BlockSpec(memory_space=pltpu.SMEM)
VMEM = pl.BlockSpec(memory_space=pltpu.VMEM)
ANY = pl.BlockSpec(memory_space=pl.ANY)
HBM = pl.BlockSpec(memory_space=pltpu.HBM)
PARAMS = pltpu.CompilerParams(vmem_limit_bytes=LIMIT)


def row_code(peak):
    return jnp.ceil(jnp.log2(jnp.maximum(peak, 1e-30)) * 256.0)


def to_int(x, code):
    y = jnp.round(x * (jnp.exp2(code * (-1.0 / 256.0)) * 32767.0))
    return jnp.clip(y, -32767.0, 32767.0)


def scale_of(code):
    return jnp.exp2(code * (1.0 / 256.0)) * (1.0 / 32767.0)


def as_s16(x):
    return x.astype(jnp.int32).astype(S16)


def as_f32(x):
    return x.astype(jnp.int32).astype(F32)


def row_peak(x):
    return jnp.max(jnp.abs(x), axis=-1, keepdims=True)


def lane_ids(shape):
    return lax.broadcasted_iota(jnp.int32, shape, len(shape) - 1)


def dot_nt(a, b):
    return lax.dot_general(a, b, (((1,), (1,)), ((), ())), preferred_element_type=F32)


def dot_nn(a, b):
    return jnp.dot(a, b, preferred_element_type=F32)


def halves(x):
    high = x.astype(BF16)
    return high, (x - high.astype(F32)).astype(BF16)


def cost(flops, nbytes, exps=0):
    return pl.CostEstimate(flops=flops, bytes_accessed=nbytes, transcendentals=exps)


def place_of(ctx, count, columns):
    rest = count // columns
    return ctx % rest * columns + ctx // rest


def parcel_kernel(
    owner, member, selected, latent_t, out, lists, stage, wide, coded, ids_v, ids, in_sems, id_sems, sems, *, columns
):
    width, total = latent_t.shape
    blocks, part, padded = coded.shape
    block = total // blocks
    groups = total // LANES
    fetch = pltpu.make_async_copy(selected, lists, id_sems.at[0])
    fetch.start()
    loads = []
    for n in range(groups):
        span = pl.ds(n * LANES, LANES)
        load = pltpu.make_async_copy(latent_t.at[:, span], stage.at[:, span], in_sems.at[n])
        load.start()
        loads.append(load)
    fetch.wait()
    offset = lists[...] - owner[0] * blocks
    mine = (offset >= 0) & (offset < blocks)
    first = jnp.min(jnp.where(mine, offset, blocks), axis=1, keepdims=True)
    last = jnp.max(jnp.where(mine, offset, -1), axis=1, keepdims=True)
    ids_v[...] = jnp.where(lane_ids(ids_v.shape) == 0, first, last)
    move = pltpu.make_async_copy(ids_v, ids, id_sems.at[1])
    move.start()
    lanes = lane_ids((part, padded))
    for n in range(groups):
        loads[n].wait()
        wide[:, :width] = stage[:, n * LANES : (n + 1) * LANES].T
        for m in range(LANES // block):
            at = pl.multiple_of(m * block + member[0] * part, part)
            x = jnp.where(lanes < width, wide[pl.ds(at, part), :], 0.0)
            code = row_code(row_peak(x))
            full = jnp.where(lanes < width, to_int(x, code), code)
            coded[n * (LANES // block) + m] = as_s16(full)
    move.wait()
    copies = []
    for d in range(out.shape[0]):
        low, high = ids[d, 0], ids[d, 1]
        for s, (block_id, filled) in enumerate(((low, low <= high), (high, low < high))):
            source = coded.at[jnp.clip(block_id, 0, blocks - 1)]
            copy = pltpu.make_async_copy(source, out.at[place_of(d, out.shape[0], columns), s], sems.at[2 * d + s])
            pl.when(filled)(copy.start)
            copies.append((filled, copy))
    for filled, copy in copies:
        pl.when(filled)(copy.wait)


def make_parcels(owner, member, selected, latent_t, blocks, part, padded, columns):
    receivers = selected.shape[0]
    width, total = latent_t.shape
    return pl.pallas_call(
        functools.partial(parcel_kernel, columns=columns),
        out_shape=jax.ShapeDtypeStruct((receivers, 2, part, padded), S16),
        in_specs=[SMEM, SMEM, HBM, HBM],
        out_specs=HBM,
        scratch_shapes=[
            pltpu.VMEM(selected.shape, jnp.int32),
            pltpu.VMEM((width, total), F32),
            pltpu.VMEM((LANES, padded), F32),
            pltpu.VMEM((blocks, part, padded), S16),
            pltpu.VMEM((receivers, LANES), jnp.int32),
            pltpu.SMEM((receivers, LANES), jnp.int32),
            pltpu.SemaphoreType.DMA((total // LANES,)),
            pltpu.SemaphoreType.DMA((2,)),
            pltpu.SemaphoreType.DMA((2 * receivers,)),
        ],
        compiler_params=pltpu.CompilerParams(vmem_limit_bytes=WHOLE),
        cost_estimate=cost(10**7, 4 * 10**6),
        name="parcels",
    )(owner, member, selected, latent_t)


def pack_kernel(q, out):
    rows, width = q.shape
    main = width // LANES
    code = row_code(row_peak(jnp.max(jnp.abs(q[...]), axis=0, keepdims=True)))
    for t in range(main):
        out[t * rows : (t + 1) * rows, :] = as_s16(to_int(q[:, t * LANES : (t + 1) * LANES], code))
    rest = to_int(q[:, main * LANES :], code)
    both = jnp.concatenate([rest[: rows // 2], rest[rows // 2 :]], axis=-1)
    out[main * rows : main * rows + rows // 2, :] = as_s16(both)
    out[main * rows + rows // 2 :, :] = as_s16(jnp.broadcast_to(code, (16, LANES)))


def pack_queries(q):
    rows, width = q.shape
    return pl.pallas_call(
        pack_kernel,
        out_shape=jax.ShapeDtypeStruct((rows * width // LANES + 16, LANES), S16),
        in_specs=[VMEM],
        out_specs=VMEM,
        compiler_params=PARAMS,
        cost_estimate=cost(10**7, 2 * 10**6),
        name="pack_queries",
    )(q)


def load_queries(place, half, own, other, q_s):
    some = q_s.shape[0] // PAIR
    lat = (q_s.shape[1] - 2 * LANES) // 2
    rows = PAIR * some
    turn = place[1] if half == 1 else 1 - place[1]
    lanes = lane_ids((some, LANES))
    for n, q in enumerate((own, other)):
        end = q.shape[0] - 16
        factor = scale_of(as_f32(q[end:, :]))[:1, :1] * (SCALE * LOG2E)
        span = slice(n * some, (n + 1) * some)
        for t in range(lat // LANES):
            at = pl.multiple_of(t * rows + turn * some, some)
            high, low = halves(as_f32(q[pl.ds(at, some), :]) * factor)
            q_s[span, t * LANES : (t + 1) * LANES] = high
            q_s[span, lat + t * LANES : lat + (t + 1) * LANES] = low
        rest = as_f32(q[end - some : end, :]) * factor
        rest = jnp.where(turn == 0, rest, pltpu.roll(rest, LANES // 2, 1))
        high, low = halves(jnp.where(lanes < LANES // 2, rest, 0.0))
        both = high.astype(F32) + pltpu.roll(low.astype(F32), LANES // 2, 1)
        q_s[span, 2 * lat : 2 * lat + LANES] = both.astype(BF16)
        q_s[span, 2 * lat + LANES :] = high


def split_kernel(place, own, other, out):
    load_queries(place, 0, own, other, out)


def split_far(place, own, other, rows, width):
    return pl.pallas_call(
        split_kernel,
        out_shape=jax.ShapeDtypeStruct((rows, width), BF16),
        in_specs=[SMEM, VMEM, VMEM],
        out_specs=VMEM,
        compiler_params=PARAMS,
        cost_estimate=cost(10**7, 4 * 10**6),
        name="split_far",
    )(place, own, other)


def half_kernel(core, values, half, sem):
    some = half.shape[0]
    copy = pltpu.make_async_copy(values.at[pl.ds(core[0] * some, some)], half, sem)
    copy.start()
    copy.wait()


def half_values(core, values):
    heads, lat, vdim = values.shape
    return pl.pallas_call(
        half_kernel,
        out_shape=jax.ShapeDtypeStruct((heads // 2, lat, vdim), BF16),
        in_specs=[SMEM, HBM],
        out_specs=VMEM,
        scratch_shapes=[pltpu.SemaphoreType.DMA],
        compiler_params=pltpu.CompilerParams(vmem_limit_bytes=WHOLE),
        cost_estimate=cost(10**4, 10**6),
        name="half_values",
    )(core, values)


def split_keys(places, arrived, keys_s):
    count = places.shape[0]
    _, part, padded = arrived.shape
    lat = padded - LANES
    rope = lane_ids((part, LANES)) < LANES // 2
    for i in range(count):
        wide = as_f32(arrived[places[i]])
        wide = wide * scale_of(wide[:, lat:])[:, LANES - 1 :]
        span = slice(i * part, (i + 1) * part)
        high, low = halves(wide[:, :lat])
        keys_s[span, :lat] = high
        keys_s[span, lat : 2 * lat] = low
        tail = jnp.where(rope, wide[:, lat:], 0.0)
        keys_s[span, 2 * lat : 2 * lat + LANES] = (tail + pltpu.roll(tail, LANES // 2, 1)).astype(BF16)
        keys_s[span, 2 * lat + LANES :] = halves(tail)[1]


def attend_rows(block_ids, place, half, q, keys_s, vp_own, fetched, passed, out, mixed_s, stat_s):
    heads, lat, vdim = vp_own.shape
    count = block_ids.shape[0]
    part = out.shape[0]
    some = fetched.shape[0]
    keys = keys_s.shape[0]
    lane = lane_ids((1, keys))
    room = jnp.zeros((1, keys), jnp.int32)
    for i in range(count):
        room = jnp.where(lane // part == i, (place[2] - block_ids[i]) * (PAIR * part), room)
    if half == 0:
        room = room + (1 - 2 * place[1]) * part
    room = room - lane % part
    spot = lax.broadcasted_iota(jnp.int32, (q.shape[0], 1), 0) // heads % part
    s = (
        dot_nt(q[:, :lat], keys_s[:, :lat])
        + dot_nt(q[:, lat : 2 * lat], keys_s[:, :lat])
        + dot_nt(q[:, :lat], keys_s[:, lat : 2 * lat])
        + dot_nt(q[:, 2 * lat :], keys_s[:, 2 * lat :])
    )
    s = jnp.where(room + spot >= 0, s, NEG)
    peak = jnp.max(s, axis=-1, keepdims=True)
    p = jnp.exp2(s - peak)
    norm = jnp.sum(p, axis=-1, keepdims=True)
    high, low = halves(p)
    mixed = dot_nn(high, keys_s[:, :lat]) + dot_nn(high, keys_s[:, lat : 2 * lat]) + dot_nn(low, keys_s[:, :lat])
    mixed = mixed / norm
    for t in range(lat // LANES):
        mixed_s[t] = mixed[:, t * LANES : (t + 1) * LANES]
    stat_s[...] = jnp.broadcast_to((peak + jnp.log2(norm)) * 2.0, stat_s.shape)
    results, stats = [], []
    for n in range(PAIR * heads):
        head = n if n < heads else heads * part + ((n - heads) // some + place[0]) % 2 * some + n % some
        rows = pl.ds(head, part, stride=heads)
        high, low = halves(jnp.concatenate([mixed_s[t, rows, :] for t in range(lat // LANES)], axis=-1))
        maps = vp_own[n] if n < heads else (fetched[n - heads] if n < heads + some else passed[n - heads - some])
        both = dot_nn(jnp.concatenate([high, low], axis=0), maps)
        results.append(both[:part] + both[part:])
        stats.append(stat_s[rows, :])
    head_out = jnp.concatenate(results, axis=-1)
    code = row_code(row_peak(head_out))
    inner = head_out.shape[-1]
    coded = as_s16(to_int(head_out, code))
    half = inner // PAIR
    width = some * vdim
    out[:, :half] = coded[:, :half]
    for n, turn in enumerate((place[0], 1 - place[0])):
        at = pl.multiple_of(half + turn * width, width)
        out[:, pl.ds(at, width)] = coded[:, half + n * width : half + (n + 1) * width]
    lane = lane_ids((part, LANES))
    tail = code
    for n in range(PAIR * heads):
        at = n
        if n >= heads:
            turn = place[0] if n < heads + some else 1 - place[0]
            at = heads + turn * some + n % some
        coarse = jnp.floor(stats[n])
        tail = jnp.where(lane == at, coarse, tail)
        tail = jnp.where(lane == at + PAIR * heads, (stats[n] - coarse) * 32767.0, tail)
    out[:, inner:] = as_s16(tail)


def far_kernel(
    places, block_ids, place, q, arrived, vp_own, fetched, passed, out, keys_s, mixed_s, stat_s
):
    split_keys(places, arrived, keys_s)
    attend_rows(block_ids, place, 0, q, keys_s, vp_own, fetched, passed, out, mixed_s, stat_s)


def near_kernel(block_ids, place, own, other, keys_s, vp_own, fetched, passed, out, q_s, mixed_s, stat_s):
    load_queries(place, 1, own, other, q_s)
    attend_rows(block_ids, place, 1, q_s, keys_s, vp_own, fetched, passed, out, mixed_s, stat_s)


def attend_far(places, block_ids, place, q, arrived, vp_own, fetched, passed):
    count = places.shape[0]
    _, part, padded = arrived.shape
    heads, lat, vdim = vp_own.shape
    rows = PAIR * heads * part
    return pl.pallas_call(
        far_kernel,
        out_shape=(
            jax.ShapeDtypeStruct((part, PAIR * heads * vdim + LANES), S16),
            jax.ShapeDtypeStruct((count * part, 2 * padded), BF16),
        ),
        in_specs=[SMEM, SMEM, SMEM] + [VMEM] * 5,
        out_specs=(VMEM, VMEM),
        scratch_shapes=[
            pltpu.VMEM((lat // LANES, rows, LANES), F32),
            pltpu.VMEM((rows, LANES), F32),
        ],
        compiler_params=PARAMS,
        cost_estimate=cost(4 * 10**9, 6 * 10**6, 10**6),
        name="attend_far",
    )(places, block_ids, place, q, arrived, vp_own, fetched, passed)


def attend_near(block_ids, place, own, other, keys, vp_own, fetched, passed, part):
    heads, lat, vdim = vp_own.shape
    rows = PAIR * heads * part
    return pl.pallas_call(
        near_kernel,
        out_shape=jax.ShapeDtypeStruct((part, PAIR * heads * vdim + LANES), S16),
        in_specs=[SMEM, SMEM, VMEM, VMEM, VMEM, VMEM, VMEM, VMEM],
        out_specs=VMEM,
        scratch_shapes=[
            pltpu.VMEM((rows, keys.shape[1]), BF16),
            pltpu.VMEM((lat // LANES, rows, LANES), F32),
            pltpu.VMEM((rows, LANES), F32),
        ],
        compiler_params=PARAMS,
        cost_estimate=cost(4 * 10**9, 6 * 10**6, 10**6),
        name="attend_near",
    )(block_ids, place, own, other, keys, vp_own, fetched, passed)


def merge_kernel(place, here, there, out, *, heads):
    rows, padded = here.shape
    inner = padded - LANES
    width = inner // PAIR
    vdim = width // heads
    tails = [as_f32(x[:, inner:]) for x in (here, there)]
    logs = [(x + pltpu.roll(x, LANES - PAIR * heads, 1) * (1.0 / 32767.0)) * 0.5 for x in tails]
    scales = [scale_of(x)[:, LANES - 1 :] for x in tails]
    merged = []
    for g in range(PAIR):
        a = logs[0] if g == 0 else pltpu.roll(logs[0], LANES - heads, 1)
        b = logs[1] if g == 1 else pltpu.roll(logs[1], LANES - heads, 1)
        top = jnp.maximum(a, b)
        a, b = jnp.exp2(a - top), jnp.exp2(b - top)
        total = a + b
        a, b = a / total * scales[0], b / total * scales[1]
        for h in range(heads):
            x = as_f32(here[:, g * width + h * vdim : g * width + (h + 1) * vdim]) * a[:, h : h + 1]
            y = as_f32(there[:, (1 - g) * width + h * vdim : (1 - g) * width + (h + 1) * vdim]) * b[:, h : h + 1]
            merged.append((x + y).astype(BF16).astype(F32))
    head_out = jnp.concatenate(merged, axis=-1)
    code = row_code(row_peak(head_out))
    coded = as_s16(to_int(head_out, code))
    for g, turn in enumerate((place[1], 1 - place[1])):
        out[:, pl.ds(pl.multiple_of(turn * width, width), width)] = coded[:, g * width : (g + 1) * width]
    out[:, inner:] = as_s16(jnp.broadcast_to(code, (rows, LANES)))


def merge(place, here, there, heads):
    return pl.pallas_call(
        functools.partial(merge_kernel, heads=heads),
        out_shape=jax.ShapeDtypeStruct(here.shape, S16),
        in_specs=[SMEM, VMEM, VMEM],
        out_specs=VMEM,
        compiler_params=PARAMS,
        cost_estimate=cost(10**6, 5 * 10**5),
        name="merge",
    )(place, here, there)


def project_kernel(place, rows_in, near_own, near_other, far_own, far_other, out, wide):
    chips, rows, padded = rows_in.shape
    inner = padded - LANES
    columns, depth = near_own.shape
    core = place[0]
    factor = scale_of(as_f32(rows_in[:, :, inner:]).reshape(chips * rows, LANES))[:, :1]
    sums = [None, None]
    for n, member in enumerate((place[1], 1 - place[1])):
        at = pl.multiple_of(member * depth, depth)
        a = as_f32(rows_in[:, :, pl.ds(at, depth)]).reshape(chips * rows, depth)
        a = (a * factor).astype(BF16)
        for k, weights in enumerate(((near_own, far_own), (near_other, far_other))[n]):
            term = dot_nt(a, weights[...])
            sums[k] = term if n == 0 else sums[k] + term
    spare = 2 * LANES - columns
    keep = LANES - spare
    groups = rows // 8
    for k, at in enumerate((core, 1 - core)):
        wide[:, :columns] = sums[k]
        out[at, :, :rows, :] = wide[:, :LANES].reshape(chips, rows, LANES).astype(BF16)
        rest = wide[:, LANES:].reshape(chips, groups, 8, LANES)
        last = rest[:, groups - 1].reshape(chips * 8, LANES)
        lanes = lane_ids(last.shape)
        packed = []
        for g in range(groups - 1):
            moved = pltpu.roll(last, (keep - spare * g) % LANES, 1)
            packed.append(jnp.where(lanes < keep, rest[:, g].reshape(chips * 8, LANES), moved))
        packed = jnp.concatenate([x.reshape(chips, 8, LANES) for x in packed], axis=1)
        out[at, :, rows:, :] = packed.astype(BF16)


def project(place, rows_in, near_own, near_other, far_own, far_other):
    chips, rows, _ = rows_in.shape
    return pl.pallas_call(
        project_kernel,
        out_shape=jax.ShapeDtypeStruct((2, chips, rows * near_own.shape[0] // LANES, LANES), BF16),
        in_specs=[SMEM] + [VMEM] * 5,
        out_specs=VMEM,
        scratch_shapes=[pltpu.VMEM((chips * rows, 2 * LANES), F32)],
        compiler_params=PARAMS,
        cost_estimate=cost(10**9, 7 * 10**6),
        name="project",
    )(place, rows_in, near_own, near_other, far_own, far_other)


def add_kernel(parts, out):
    cores, outer, groups, packed, _ = parts.shape
    columns, total = out.shape
    rows = total // (cores * groups)
    spare = 2 * LANES - columns
    keep = LANES - spare
    lanes = lane_ids((8, LANES))
    left, right = [], []
    for k in range(cores):
        for g in range(groups):
            full = parts[k, 0, g].astype(F32)
            for z in range(1, outer):
                full = full + parts[k, z, g].astype(F32)
            left.append(full[:rows])
            pieces = [full[rows + 8 * n : rows + 8 * (n + 1)] for n in range(rows // 8 - 1)]
            last = jnp.zeros((8, LANES), F32)
            for n, piece in enumerate(pieces):
                moved = pltpu.roll(piece, (spare * n - keep) % LANES, 1)
                last = jnp.where((lanes >= spare * n) & (lanes < spare * (n + 1)), moved, last)
            right.extend(pieces + [last])
    out[:LANES, :] = jnp.concatenate(left, axis=0).T.astype(BF16)
    out[LANES:, :] = jnp.concatenate(right, axis=0).T[: columns - LANES].astype(BF16)


def add_parts(parts, columns):
    cores, _, groups, packed, _ = parts.shape
    rows = packed * LANES // columns
    return pl.pallas_call(
        add_kernel,
        out_shape=jax.ShapeDtypeStruct((columns, cores * groups * rows), BF16),
        in_specs=[VMEM],
        out_specs=VMEM,
        compiler_params=PARAMS,
        cost_estimate=cost(10**6, 10**6),
        name="add_parts",
    )(parts)


def on_device(queries, latent, selected, value_proj, out_proj):
    plane = ("x", "y", "core")
    ctx_count = lax.axis_size(plane)
    ctx_index = lax.axis_index(plane)
    core = lax.axis_index("core").astype(jnp.int32)
    member = lax.axis_index("zb").astype(jnp.int32)
    block, heads, width = queries.shape
    per_owner = latent.shape[0] // block
    key_blocks = per_owner * ctx_count
    padded = -(-width // LANES) * LANES
    columns = out_proj.shape[1]
    part = block // PAIR
    swap = [(0, 1), (1, 0)]

    parcels = make_parcels(ctx_index[None].astype(jnp.int32), member[None], selected, latent.T, per_owner, part, padded, lax.axis_size("x"))
    parcels, queries, value_near = lax.optimization_barrier((parcels, queries, value_proj))
    arrived = lax.all_to_all(parcels, ("y", "core", "x"), split_axis=0, concat_axis=0, tiled=True)

    q = queries.reshape(block * heads, width)
    near_own = out_proj.T
    q_own = pack_queries(q)
    q_other = lax.ppermute(q_own, "zb", swap)
    near_own = lax.optimization_barrier((q_own, near_own))[1]
    far_own = lax.ppermute(near_own, "core", swap)
    place = jnp.stack([core, member, key_blocks - ctx_count + ctx_index]).astype(jnp.int32)

    fetched = lax.ppermute(half_values(core[None], value_near), "zb", swap)
    passed = lax.ppermute(fetched, "core", swap)
    listed = lax.optimization_barrier((fetched, selected))[1]
    own_list = lax.dynamic_slice_in_dim(listed, ctx_index, 1, 0)[0]
    owner = own_list // per_owner
    second = jnp.any((owner[None, :] == owner[:, None]) & (own_list[None, :] < own_list[:, None]), axis=1)
    places = place_of(owner, ctx_count, lax.axis_size("x")) * 2 + second.astype(jnp.int32)

    slab = lax.optimization_barrier((fetched, near_own))[1]
    near_other = lax.ppermute(slab, "zb", swap)
    arrived = arrived.reshape(2 * ctx_count, part, padded)
    arrived, q_own, q_other = lax.optimization_barrier((arrived, q_own, q_other))
    q_far = split_far(place, q_own, q_other, heads * block, 2 * padded)
    for_partner, keys = attend_far(places, own_list, place, q_far, arrived, value_proj, fetched, passed)
    there = lax.ppermute(for_partner, "zb", swap)
    here = attend_near(own_list, place, q_own, q_other, keys, value_proj, fetched, passed, part)
    here, near_other = lax.optimization_barrier((here, near_other))
    far_other = lax.ppermute(near_other, "core", swap)
    gathered = lax.all_gather(merge(place, here, there, heads), ("x", "y"), axis=0, tiled=False)
    partial = project(place, gathered, near_own, near_other, far_own, far_other)
    partial = partial.reshape(-1, *partial.shape[2:])
    sent = lax.all_to_all(partial, ("core", "zq", "zb"), split_axis=0, concat_axis=0, tiled=True)
    return add_parts(sent.reshape(2, -1, PAIR, *sent.shape[1:]), columns).T


def solution(mesh):
    shape = (4, 4, 2, mesh.shape["head"] // PAIR, PAIR)
    fine = Mesh(mesh.devices.reshape(shape), ("x", "y", "core", "zq", "zb"))
    ctx, head = ("x", "y", "core"), ("zq", "zb")
    in_specs = (
        P(ctx, head, None),
        P(ctx, None),
        P(),
        P(head, None, None),
        P(head, ctx),
    )
    return jax.shard_map(on_device, mesh=fine, in_specs=in_specs, out_specs=P(head, ctx), check_vma=False)
```

```python
import functools
import math

import jax
import jax.numpy as jnp
from jax import lax
from jax.experimental import pallas as pl
from jax.experimental.pallas import tpu as pltpu
from jax.sharding import Mesh
from jax.sharding import PartitionSpec as P

NEG = -1e30
SCALE = 1.0 / 192.0**0.5
LOG2E = math.log2(math.e)
F32, BF16, S16 = jnp.float32, jnp.bfloat16, jnp.int16
LANES = 128
PAIR = 2
LIMIT = 32 * 1024 * 1024
WHOLE = 60 * 1024 * 1024
SMEM = pl.BlockSpec(memory_space=pltpu.SMEM)
VMEM = pl.BlockSpec(memory_space=pltpu.VMEM)
ANY = pl.BlockSpec(memory_space=pl.ANY)
HBM = pl.BlockSpec(memory_space=pltpu.HBM)
PARAMS = pltpu.CompilerParams(vmem_limit_bytes=LIMIT)


def row_code(peak):
    return jnp.ceil(jnp.log2(jnp.maximum(peak, 1e-30)) * 256.0)


def to_int(x, code):
    y = jnp.round(x * (jnp.exp2(code * (-1.0 / 256.0)) * 32767.0))
    return jnp.clip(y, -32767.0, 32767.0)


def scale_of(code):
    return jnp.exp2(code * (1.0 / 256.0)) * (1.0 / 32767.0)


def as_s16(x):
    return x.astype(jnp.int32).astype(S16)


def as_f32(x):
    return x.astype(jnp.int32).astype(F32)


def row_peak(x):
    return jnp.max(jnp.abs(x), axis=-1, keepdims=True)


def lane_ids(shape):
    return lax.broadcasted_iota(jnp.int32, shape, len(shape) - 1)


def dot_nt(a, b):
    return lax.dot_general(a, b, (((1,), (1,)), ((), ())), preferred_element_type=F32)


def dot_nn(a, b):
    return jnp.dot(a, b, preferred_element_type=F32)


def halves(x):
    high = x.astype(BF16)
    return high, (x - high.astype(F32)).astype(BF16)


def cost(flops, nbytes, exps=0):
    return pl.CostEstimate(flops=flops, bytes_accessed=nbytes, transcendentals=exps)


def place_of(ctx, count, columns):
    rest = count // columns
    return ctx % rest * columns + ctx // rest


def parcel_kernel(
    owner, member, selected, latent_t, out, lists, stage, wide, coded, ids_v, ids, in_sems, id_sems, sems, *, columns
):
    width, total = latent_t.shape
    blocks, part, padded = coded.shape
    block = total // blocks
    groups = total // LANES
    fetch = pltpu.make_async_copy(selected, lists, id_sems.at[0])
    fetch.start()
    loads = []
    for n in range(groups):
        span = pl.ds(n * LANES, LANES)
        load = pltpu.make_async_copy(latent_t.at[:, span], stage.at[:, span], in_sems.at[n])
        load.start()
        loads.append(load)
    fetch.wait()
    offset = lists[...] - owner[0] * blocks
    mine = (offset >= 0) & (offset < blocks)
    first = jnp.min(jnp.where(mine, offset, blocks), axis=1, keepdims=True)
    last = jnp.max(jnp.where(mine, offset, -1), axis=1, keepdims=True)
    ids_v[...] = jnp.where(lane_ids(ids_v.shape) == 0, first, last)
    move = pltpu.make_async_copy(ids_v, ids, id_sems.at[1])
    move.start()
    lanes = lane_ids((part, padded))
    for n in range(groups):
        loads[n].wait()
        wide[:, :width] = stage[:, n * LANES : (n + 1) * LANES].T
        for m in range(LANES // block):
            at = pl.multiple_of(m * block + member[0] * part, part)
            x = jnp.where(lanes < width, wide[pl.ds(at, part), :], 0.0)
            code = row_code(row_peak(x))
            full = jnp.where(lanes < width, to_int(x, code), code)
            coded[n * (LANES // block) + m] = as_s16(full)
    move.wait()
    copies = []
    for d in range(out.shape[0]):
        low, high = ids[d, 0], ids[d, 1]
        for s, (block_id, filled) in enumerate(((low, low <= high), (high, low < high))):
            source = coded.at[jnp.clip(block_id, 0, blocks - 1)]
            copy = pltpu.make_async_copy(source, out.at[place_of(d, out.shape[0], columns), s], sems.at[2 * d + s])
            pl.when(filled)(copy.start)
            copies.append((filled, copy))
    for filled, copy in copies:
        pl.when(filled)(copy.wait)


def make_parcels(owner, member, selected, latent_t, blocks, part, padded, columns):
    receivers = selected.shape[0]
    width, total = latent_t.shape
    return pl.pallas_call(
        functools.partial(parcel_kernel, columns=columns),
        out_shape=jax.ShapeDtypeStruct((receivers, 2, part, padded), S16),
        in_specs=[SMEM, SMEM, HBM, HBM],
        out_specs=HBM,
        scratch_shapes=[
            pltpu.VMEM(selected.shape, jnp.int32),
            pltpu.VMEM((width, total), F32),
            pltpu.VMEM((LANES, padded), F32),
            pltpu.VMEM((blocks, part, padded), S16),
            pltpu.VMEM((receivers, LANES), jnp.int32),
            pltpu.SMEM((receivers, LANES), jnp.int32),
            pltpu.SemaphoreType.DMA((total // LANES,)),
            pltpu.SemaphoreType.DMA((2,)),
            pltpu.SemaphoreType.DMA((2 * receivers,)),
        ],
        compiler_params=pltpu.CompilerParams(vmem_limit_bytes=WHOLE),
        cost_estimate=cost(10**7, 4 * 10**6),
        name="parcels",
    )(owner, member, selected, latent_t)


def pack_kernel(q, out):
    rows, width = q.shape
    main = width // LANES
    code = row_code(row_peak(jnp.max(jnp.abs(q[...]), axis=0, keepdims=True)))
    for t in range(main):
        out[t * rows : (t + 1) * rows, :] = as_s16(to_int(q[:, t * LANES : (t + 1) * LANES], code))
    rest = to_int(q[:, main * LANES :], code)
    both = jnp.concatenate([rest[: rows // 2], rest[rows // 2 :]], axis=-1)
    out[main * rows : main * rows + rows // 2, :] = as_s16(both)
    out[main * rows + rows // 2 :, :] = as_s16(jnp.broadcast_to(code, (16, LANES)))


def pack_queries(q):
    rows, width = q.shape
    return pl.pallas_call(
        pack_kernel,
        out_shape=jax.ShapeDtypeStruct((rows * width // LANES + 16, LANES), S16),
        in_specs=[VMEM],
        out_specs=VMEM,
        compiler_params=PARAMS,
        cost_estimate=cost(10**7, 2 * 10**6),
        name="pack_queries",
    )(q)


def load_queries(place, half, own, other, q_s):
    some = q_s.shape[0] // PAIR
    lat = (q_s.shape[1] - 2 * LANES) // 2
    rows = PAIR * some
    turn = place[1] if half == 1 else 1 - place[1]
    lanes = lane_ids((some, LANES))
    for n, q in enumerate((own, other)):
        end = q.shape[0] - 16
        factor = scale_of(as_f32(q[end:, :]))[:1, :1] * (SCALE * LOG2E)
        span = slice(n * some, (n + 1) * some)
        for t in range(lat // LANES):
            at = pl.multiple_of(t * rows + turn * some, some)
            high, low = halves(as_f32(q[pl.ds(at, some), :]) * factor)
            q_s[span, t * LANES : (t + 1) * LANES] = high
            q_s[span, lat + t * LANES : lat + (t + 1) * LANES] = low
        rest = as_f32(q[end - some : end, :]) * factor
        rest = jnp.where(turn == 0, rest, pltpu.roll(rest, LANES // 2, 1))
        high, low = halves(jnp.where(lanes < LANES // 2, rest, 0.0))
        both = high.astype(F32) + pltpu.roll(low.astype(F32), LANES // 2, 1)
        q_s[span, 2 * lat : 2 * lat + LANES] = both.astype(BF16)
        q_s[span, 2 * lat + LANES :] = high


def split_kernel(place, own, other, out):
    load_queries(place, 0, own, other, out)


def split_far(place, own, other, rows, width):
    return pl.pallas_call(
        split_kernel,
        out_shape=jax.ShapeDtypeStruct((rows, width), BF16),
        in_specs=[SMEM, VMEM, VMEM],
        out_specs=VMEM,
        compiler_params=PARAMS,
        cost_estimate=cost(10**7, 4 * 10**6),
        name="split_far",
    )(place, own, other)


def half_kernel(core, values, half, sem):
    some = half.shape[0]
    copy = pltpu.make_async_copy(values.at[pl.ds(core[0] * some, some)], half, sem)
    copy.start()
    copy.wait()


def half_values(core, values):
    heads, lat, vdim = values.shape
    return pl.pallas_call(
        half_kernel,
        out_shape=jax.ShapeDtypeStruct((heads // 2, lat, vdim), BF16),
        in_specs=[SMEM, HBM],
        out_specs=VMEM,
        scratch_shapes=[pltpu.SemaphoreType.DMA],
        compiler_params=pltpu.CompilerParams(vmem_limit_bytes=WHOLE),
        cost_estimate=cost(10**4, 10**6),
        name="half_values",
    )(core, values)


def split_keys(places, arrived, keys_s):
    count = places.shape[0]
    _, part, padded = arrived.shape
    lat = padded - LANES
    rope = lane_ids((part, LANES)) < LANES // 2
    for i in range(count):
        wide = as_f32(arrived[places[i]])
        wide = wide * scale_of(wide[:, lat:])[:, LANES - 1 :]
        span = slice(i * part, (i + 1) * part)
        high, low = halves(wide[:, :lat])
        keys_s[span, :lat] = high
        keys_s[span, lat : 2 * lat] = low
        tail = jnp.where(rope, wide[:, lat:], 0.0)
        keys_s[span, 2 * lat : 2 * lat + LANES] = (tail + pltpu.roll(tail, LANES // 2, 1)).astype(BF16)
        keys_s[span, 2 * lat + LANES :] = halves(tail)[1]


def attend_rows(block_ids, place, half, q, keys_s, vp_own, fetched, passed, out, mixed_s, stat_s):
    heads, lat, vdim = vp_own.shape
    count = block_ids.shape[0]
    part = out.shape[0]
    some = fetched.shape[0]
    keys = keys_s.shape[0]
    lane = lane_ids((1, keys))
    room = jnp.zeros((1, keys), jnp.int32)
    for i in range(count):
        room = jnp.where(lane // part == i, (place[2] - block_ids[i]) * (PAIR * part), room)
    if half == 0:
        room = room + (1 - 2 * place[1]) * part
    room = room - lane % part
    spot = lax.broadcasted_iota(jnp.int32, (q.shape[0], 1), 0) // heads % part
    s = (
        dot_nt(q[:, :lat], keys_s[:, :lat])
        + dot_nt(q[:, lat : 2 * lat], keys_s[:, :lat])
        + dot_nt(q[:, :lat], keys_s[:, lat : 2 * lat])
        + dot_nt(q[:, 2 * lat :], keys_s[:, 2 * lat :])
    )
    s = jnp.where(room + spot >= 0, s, NEG)
    peak = jnp.max(s, axis=-1, keepdims=True)
    p = jnp.exp2(s - peak)
    high = p.astype(BF16)
    norm = jnp.sum(high.astype(F32), axis=-1, keepdims=True)
    mixed = dot_nn(high, keys_s[:, :lat]) + dot_nn(high, keys_s[:, lat : 2 * lat])
    mixed = mixed / norm
    for t in range(lat // LANES):
        mixed_s[t] = mixed[:, t * LANES : (t + 1) * LANES]
    stat_s[...] = jnp.broadcast_to((peak + jnp.log2(norm)) * 2.0, stat_s.shape)
    results, stats = [], []
    for n in range(PAIR * heads):
        head = n if n < heads else heads * part + ((n - heads) // some + place[0]) % 2 * some + n % some
        rows = pl.ds(head, part, stride=heads)
        high, low = halves(jnp.concatenate([mixed_s[t, rows, :] for t in range(lat // LANES)], axis=-1))
        maps = vp_own[n] if n < heads else (fetched[n - heads] if n < heads + some else passed[n - heads - some])
        both = dot_nn(jnp.concatenate([high, low], axis=0), maps)
        results.append(both[:part] + both[part:])
        stats.append(stat_s[rows, :])
    head_out = jnp.concatenate(results, axis=-1)
    code = row_code(row_peak(head_out))
    inner = head_out.shape[-1]
    coded = as_s16(to_int(head_out, code))
    half = inner // PAIR
    width = some * vdim
    out[:, :half] = coded[:, :half]
    for n, turn in enumerate((place[0], 1 - place[0])):
        at = pl.multiple_of(half + turn * width, width)
        out[:, pl.ds(at, width)] = coded[:, half + n * width : half + (n + 1) * width]
    lane = lane_ids((part, LANES))
    tail = code
    for n in range(PAIR * heads):
        at = n
        if n >= heads:
            turn = place[0] if n < heads + some else 1 - place[0]
            at = heads + turn * some + n % some
        coarse = jnp.floor(stats[n])
        tail = jnp.where(lane == at, coarse, tail)
        tail = jnp.where(lane == at + PAIR * heads, (stats[n] - coarse) * 32767.0, tail)
    out[:, inner:] = as_s16(tail)


def far_kernel(
    places, block_ids, place, q, arrived, vp_own, fetched, passed, out, keys_s, mixed_s, stat_s
):
    split_keys(places, arrived, keys_s)
    attend_rows(block_ids, place, 0, q, keys_s, vp_own, fetched, passed, out, mixed_s, stat_s)


def near_kernel(block_ids, place, own, other, keys_s, vp_own, fetched, passed, out, q_s, mixed_s, stat_s):
    load_queries(place, 1, own, other, q_s)
    attend_rows(block_ids, place, 1, q_s, keys_s, vp_own, fetched, passed, out, mixed_s, stat_s)


def attend_far(places, block_ids, place, q, arrived, vp_own, fetched, passed):
    count = places.shape[0]
    _, part, padded = arrived.shape
    heads, lat, vdim = vp_own.shape
    rows = PAIR * heads * part
    return pl.pallas_call(
        far_kernel,
        out_shape=(
            jax.ShapeDtypeStruct((part, PAIR * heads * vdim + LANES), S16),
            jax.ShapeDtypeStruct((count * part, 2 * padded), BF16),
        ),
        in_specs=[SMEM, SMEM, SMEM] + [VMEM] * 5,
        out_specs=(VMEM, VMEM),
        scratch_shapes=[
            pltpu.VMEM((lat // LANES, rows, LANES), F32),
            pltpu.VMEM((rows, LANES), F32),
        ],
        compiler_params=PARAMS,
        cost_estimate=cost(4 * 10**9, 6 * 10**6, 10**6),
        name="attend_far",
    )(places, block_ids, place, q, arrived, vp_own, fetched, passed)


def attend_near(block_ids, place, own, other, keys, vp_own, fetched, passed, part):
    heads, lat, vdim = vp_own.shape
    rows = PAIR * heads * part
    return pl.pallas_call(
        near_kernel,
        out_shape=jax.ShapeDtypeStruct((part, PAIR * heads * vdim + LANES), S16),
        in_specs=[SMEM, SMEM, VMEM, VMEM, VMEM, VMEM, VMEM, VMEM],
        out_specs=VMEM,
        scratch_shapes=[
            pltpu.VMEM((rows, keys.shape[1]), BF16),
            pltpu.VMEM((lat // LANES, rows, LANES), F32),
            pltpu.VMEM((rows, LANES), F32),
        ],
        compiler_params=PARAMS,
        cost_estimate=cost(4 * 10**9, 6 * 10**6, 10**6),
        name="attend_near",
    )(block_ids, place, own, other, keys, vp_own, fetched, passed)


def merge_kernel(place, here, there, out, *, heads):
    rows, padded = here.shape
    inner = padded - LANES
    width = inner // PAIR
    vdim = width // heads
    tails = [as_f32(x[:, inner:]) for x in (here, there)]
    logs = [(x + pltpu.roll(x, LANES - PAIR * heads, 1) * (1.0 / 32767.0)) * 0.5 for x in tails]
    scales = [scale_of(x)[:, LANES - 1 :] for x in tails]
    merged = []
    for g in range(PAIR):
        a = logs[0] if g == 0 else pltpu.roll(logs[0], LANES - heads, 1)
        b = logs[1] if g == 1 else pltpu.roll(logs[1], LANES - heads, 1)
        top = jnp.maximum(a, b)
        a, b = jnp.exp2(a - top), jnp.exp2(b - top)
        total = a + b
        a, b = a / total * scales[0], b / total * scales[1]
        for h in range(heads):
            x = as_f32(here[:, g * width + h * vdim : g * width + (h + 1) * vdim]) * a[:, h : h + 1]
            y = as_f32(there[:, (1 - g) * width + h * vdim : (1 - g) * width + (h + 1) * vdim]) * b[:, h : h + 1]
            merged.append((x + y).astype(BF16).astype(F32))
    head_out = jnp.concatenate(merged, axis=-1)
    code = row_code(row_peak(head_out))
    coded = as_s16(to_int(head_out, code))
    for g, turn in enumerate((place[1], 1 - place[1])):
        out[:, pl.ds(pl.multiple_of(turn * width, width), width)] = coded[:, g * width : (g + 1) * width]
    out[:, inner:] = as_s16(jnp.broadcast_to(code, (rows, LANES)))


def merge(place, here, there, heads):
    return pl.pallas_call(
        functools.partial(merge_kernel, heads=heads),
        out_shape=jax.ShapeDtypeStruct(here.shape, S16),
        in_specs=[SMEM, VMEM, VMEM],
        out_specs=VMEM,
        compiler_params=PARAMS,
        cost_estimate=cost(10**6, 5 * 10**5),
        name="merge",
    )(place, here, there)


def project_kernel(place, rows_in, near_own, near_other, far_own, far_other, out, wide):
    chips, rows, padded = rows_in.shape
    inner = padded - LANES
    columns, depth = near_own.shape
    core = place[0]
    factor = scale_of(as_f32(rows_in[:, :, inner:]).reshape(chips * rows, LANES))[:, :1]
    sums = [None, None]
    for n, member in enumerate((place[1], 1 - place[1])):
        at = pl.multiple_of(member * depth, depth)
        a = as_f32(rows_in[:, :, pl.ds(at, depth)]).reshape(chips * rows, depth)
        a = (a * factor).astype(BF16)
        for k, weights in enumerate(((near_own, far_own), (near_other, far_other))[n]):
            term = dot_nt(a, weights[...])
            sums[k] = term if n == 0 else sums[k] + term
    spare = 2 * LANES - columns
    keep = LANES - spare
    groups = rows // 8
    for k, at in enumerate((core, 1 - core)):
        wide[:, :columns] = sums[k]
        out[at, :, :rows, :] = wide[:, :LANES].reshape(chips, rows, LANES).astype(BF16)
        rest = wide[:, LANES:].reshape(chips, groups, 8, LANES)
        last = rest[:, groups - 1].reshape(chips * 8, LANES)
        lanes = lane_ids(last.shape)
        packed = []
        for g in range(groups - 1):
            moved = pltpu.roll(last, (keep - spare * g) % LANES, 1)
            packed.append(jnp.where(lanes < keep, rest[:, g].reshape(chips * 8, LANES), moved))
        packed = jnp.concatenate([x.reshape(chips, 8, LANES) for x in packed], axis=1)
        out[at, :, rows:, :] = packed.astype(BF16)


def project(place, rows_in, near_own, near_other, far_own, far_other):
    chips, rows, _ = rows_in.shape
    return pl.pallas_call(
        project_kernel,
        out_shape=jax.ShapeDtypeStruct((2, chips, rows * near_own.shape[0] // LANES, LANES), BF16),
        in_specs=[SMEM] + [VMEM] * 5,
        out_specs=VMEM,
        scratch_shapes=[pltpu.VMEM((chips * rows, 2 * LANES), F32)],
        compiler_params=PARAMS,
        cost_estimate=cost(10**9, 7 * 10**6),
        name="project",
    )(place, rows_in, near_own, near_other, far_own, far_other)


def add_kernel(parts, out):
    cores, outer, groups, packed, _ = parts.shape
    columns, total = out.shape
    rows = total // (cores * groups)
    spare = 2 * LANES - columns
    keep = LANES - spare
    lanes = lane_ids((8, LANES))
    left, right = [], []
    for k in range(cores):
        for g in range(groups):
            full = parts[k, 0, g].astype(F32)
            for z in range(1, outer):
                full = full + parts[k, z, g].astype(F32)
            left.append(full[:rows])
            pieces = [full[rows + 8 * n : rows + 8 * (n + 1)] for n in range(rows // 8 - 1)]
            last = jnp.zeros((8, LANES), F32)
            for n, piece in enumerate(pieces):
                moved = pltpu.roll(piece, (spare * n - keep) % LANES, 1)
                last = jnp.where((lanes >= spare * n) & (lanes < spare * (n + 1)), moved, last)
            right.extend(pieces + [last])
    out[:LANES, :] = jnp.concatenate(left, axis=0).T.astype(BF16)
    out[LANES:, :] = jnp.concatenate(right, axis=0).T[: columns - LANES].astype(BF16)


def add_parts(parts, columns):
    cores, _, groups, packed, _ = parts.shape
    rows = packed * LANES // columns
    return pl.pallas_call(
        add_kernel,
        out_shape=jax.ShapeDtypeStruct((columns, cores * groups * rows), BF16),
        in_specs=[VMEM],
        out_specs=VMEM,
        compiler_params=PARAMS,
        cost_estimate=cost(10**6, 10**6),
        name="add_parts",
    )(parts)


def on_device(queries, latent, selected, value_proj, out_proj):
    plane = ("x", "y", "core")
    ctx_count = lax.axis_size(plane)
    ctx_index = lax.axis_index(plane)
    core = lax.axis_index("core").astype(jnp.int32)
    member = lax.axis_index("zb").astype(jnp.int32)
    block, heads, width = queries.shape
    per_owner = latent.shape[0] // block
    key_blocks = per_owner * ctx_count
    padded = -(-width // LANES) * LANES
    columns = out_proj.shape[1]
    part = block // PAIR
    swap = [(0, 1), (1, 0)]

    parcels = make_parcels(ctx_index[None].astype(jnp.int32), member[None], selected, latent.T, per_owner, part, padded, lax.axis_size("x"))
    parcels, queries, value_near = lax.optimization_barrier((parcels, queries, value_proj))
    arrived = lax.all_to_all(parcels, ("y", "core", "x"), split_axis=0, concat_axis=0, tiled=True)

    q = queries.reshape(block * heads, width)
    near_own = out_proj.T
    q_own = pack_queries(q)
    q_other = lax.ppermute(q_own, "zb", swap)
    near_own = lax.optimization_barrier((q_own, near_own))[1]
    far_own = lax.ppermute(near_own, "core", swap)
    place = jnp.stack([core, member, key_blocks - ctx_count + ctx_index]).astype(jnp.int32)

    fetched = lax.ppermute(half_values(core[None], value_near), "zb", swap)
    passed = lax.ppermute(fetched, "core", swap)
    listed = lax.optimization_barrier((fetched, selected))[1]
    own_list = lax.dynamic_slice_in_dim(listed, ctx_index, 1, 0)[0]
    owner = own_list // per_owner
    second = jnp.any((owner[None, :] == owner[:, None]) & (own_list[None, :] < own_list[:, None]), axis=1)
    places = place_of(owner, ctx_count, lax.axis_size("x")) * 2 + second.astype(jnp.int32)

    slab = lax.optimization_barrier((fetched, near_own))[1]
    near_other = lax.ppermute(slab, "zb", swap)
    arrived = arrived.reshape(2 * ctx_count, part, padded)
    arrived, q_own, q_other = lax.optimization_barrier((arrived, q_own, q_other))
    q_far = split_far(place, q_own, q_other, heads * block, 2 * padded)
    for_partner, keys = attend_far(places, own_list, place, q_far, arrived, value_proj, fetched, passed)
    there = lax.ppermute(for_partner, "zb", swap)
    here = attend_near(own_list, place, q_own, q_other, keys, value_proj, fetched, passed, part)
    here, near_other = lax.optimization_barrier((here, near_other))
    far_other = lax.ppermute(near_other, "core", swap)
    gathered = lax.all_gather(merge(place, here, there, heads), ("x", "y"), axis=0, tiled=False)
    partial = project(place, gathered, near_own, near_other, far_own, far_other)
    partial = partial.reshape(-1, *partial.shape[2:])
    sent = lax.all_to_all(partial, ("core", "zq", "zb"), split_axis=0, concat_axis=0, tiled=True)
    return add_parts(sent.reshape(2, -1, PAIR, *sent.shape[1:]), columns).T


def solution(mesh):
    shape = (4, 4, 2, mesh.shape["head"] // PAIR, PAIR)
    fine = Mesh(mesh.devices.reshape(shape), ("x", "y", "core", "zq", "zb"))
    ctx, head = ("x", "y", "core"), ("zq", "zb")
    in_specs = (
        P(ctx, head, None),
        P(ctx, None),
        P(),
        P(head, None, None),
        P(head, ctx),
    )
    return jax.shard_map(on_device, mesh=fine, in_specs=in_specs, out_specs=P(head, ctx), check_vma=False)
```

```python
import functools
import math

import jax
import jax.numpy as jnp
from jax import lax
from jax.experimental import pallas as pl
from jax.experimental.pallas import tpu as pltpu
from jax.sharding import Mesh
from jax.sharding import PartitionSpec as P

NEG = -1e30
SCALE = 1.0 / 192.0**0.5
LOG2E = math.log2(math.e)
F32, BF16, S16 = jnp.float32, jnp.bfloat16, jnp.int16
LANES = 128
PAIR = 2
LIMIT = 32 * 1024 * 1024
WHOLE = 60 * 1024 * 1024
SMEM = pl.BlockSpec(memory_space=pltpu.SMEM)
VMEM = pl.BlockSpec(memory_space=pltpu.VMEM)
ANY = pl.BlockSpec(memory_space=pl.ANY)
HBM = pl.BlockSpec(memory_space=pltpu.HBM)
PARAMS = pltpu.CompilerParams(vmem_limit_bytes=LIMIT)


def row_code(peak):
    return jnp.ceil(jnp.log2(jnp.maximum(peak, 1e-30)) * 256.0)


def to_int(x, code):
    y = jnp.round(x * (jnp.exp2(code * (-1.0 / 256.0)) * 32767.0))
    return jnp.clip(y, -32767.0, 32767.0)


def scale_of(code):
    return jnp.exp2(code * (1.0 / 256.0)) * (1.0 / 32767.0)


def as_s16(x):
    return x.astype(jnp.int32).astype(S16)


def as_f32(x):
    return x.astype(jnp.int32).astype(F32)


def row_peak(x):
    return jnp.max(jnp.abs(x), axis=-1, keepdims=True)


def lane_ids(shape):
    return lax.broadcasted_iota(jnp.int32, shape, len(shape) - 1)


def dot_nt(a, b):
    return lax.dot_general(a, b, (((1,), (1,)), ((), ())), preferred_element_type=F32)


def dot_nn(a, b):
    return jnp.dot(a, b, preferred_element_type=F32)


def halves(x):
    high = x.astype(BF16)
    return high, (x - high.astype(F32)).astype(BF16)


def cost(flops, nbytes, exps=0):
    return pl.CostEstimate(flops=flops, bytes_accessed=nbytes, transcendentals=exps)


def place_of(ctx, count, columns):
    rest = count // columns
    return ctx % rest * columns + ctx // rest


def parcel_kernel(
    owner, member, selected, latent_t, out, lists, stage, wide, coded, ids_v, ids, in_sems, id_sems, sems, *, columns
):
    width, total = latent_t.shape
    blocks, part, padded = coded.shape
    block = total // blocks
    groups = total // LANES
    fetch = pltpu.make_async_copy(selected, lists, id_sems.at[0])
    fetch.start()
    loads = []
    for n in range(groups):
        span = pl.ds(n * LANES, LANES)
        load = pltpu.make_async_copy(latent_t.at[:, span], stage.at[:, span], in_sems.at[n])
        load.start()
        loads.append(load)
    fetch.wait()
    offset = lists[...] - owner[0] * blocks
    mine = (offset >= 0) & (offset < blocks)
    first = jnp.min(jnp.where(mine, offset, blocks), axis=1, keepdims=True)
    last = jnp.max(jnp.where(mine, offset, -1), axis=1, keepdims=True)
    ids_v[...] = jnp.where(lane_ids(ids_v.shape) == 0, first, last)
    move = pltpu.make_async_copy(ids_v, ids, id_sems.at[1])
    move.start()
    lanes = lane_ids((part, padded))
    for n in range(groups):
        loads[n].wait()
        wide[:, :width] = stage[:, n * LANES : (n + 1) * LANES].T
        for m in range(LANES // block):
            at = pl.multiple_of(m * block + member[0] * part, part)
            x = jnp.where(lanes < width, wide[pl.ds(at, part), :], 0.0)
            code = row_code(row_peak(x))
            full = jnp.where(lanes < width, to_int(x, code), code)
            coded[n * (LANES // block) + m] = as_s16(full)
    move.wait()
    copies = []
    for d in range(out.shape[0]):
        low, high = ids[d, 0], ids[d, 1]
        for s, (block_id, filled) in enumerate(((low, low <= high), (high, low < high))):
            source = coded.at[jnp.clip(block_id, 0, blocks - 1)]
            copy = pltpu.make_async_copy(source, out.at[place_of(d, out.shape[0], columns), s], sems.at[2 * d + s])
            pl.when(filled)(copy.start)
            copies.append((filled, copy))
    for filled, copy in copies:
        pl.when(filled)(copy.wait)


def make_parcels(owner, member, selected, latent_t, blocks, part, padded, columns):
    receivers = selected.shape[0]
    width, total = latent_t.shape
    return pl.pallas_call(
        functools.partial(parcel_kernel, columns=columns),
        out_shape=jax.ShapeDtypeStruct((receivers, 2, part, padded), S16),
        in_specs=[SMEM, SMEM, HBM, HBM],
        out_specs=HBM,
        scratch_shapes=[
            pltpu.VMEM(selected.shape, jnp.int32),
            pltpu.VMEM((width, total), F32),
            pltpu.VMEM((LANES, padded), F32),
            pltpu.VMEM((blocks, part, padded), S16),
            pltpu.VMEM((receivers, LANES), jnp.int32),
            pltpu.SMEM((receivers, LANES), jnp.int32),
            pltpu.SemaphoreType.DMA((total // LANES,)),
            pltpu.SemaphoreType.DMA((2,)),
            pltpu.SemaphoreType.DMA((2 * receivers,)),
        ],
        compiler_params=pltpu.CompilerParams(vmem_limit_bytes=WHOLE),
        cost_estimate=cost(10**7, 4 * 10**6),
        name="parcels",
    )(owner, member, selected, latent_t)


def pack_kernel(q, out):
    rows, width = q.shape
    main = width // LANES
    code = row_code(row_peak(jnp.max(jnp.abs(q[...]), axis=0, keepdims=True)))
    for t in range(main):
        out[t * rows : (t + 1) * rows, :] = as_s16(to_int(q[:, t * LANES : (t + 1) * LANES], code))
    rest = to_int(q[:, main * LANES :], code)
    both = jnp.concatenate([rest[: rows // 2], rest[rows // 2 :]], axis=-1)
    out[main * rows : main * rows + rows // 2, :] = as_s16(both)
    out[main * rows + rows // 2 :, :] = as_s16(jnp.broadcast_to(code, (16, LANES)))


def pack_queries(q):
    rows, width = q.shape
    return pl.pallas_call(
        pack_kernel,
        out_shape=jax.ShapeDtypeStruct((rows * width // LANES + 16, LANES), S16),
        in_specs=[VMEM],
        out_specs=VMEM,
        compiler_params=PARAMS,
        cost_estimate=cost(10**7, 2 * 10**6),
        name="pack_queries",
    )(q)


def load_queries(place, half, own, other, q_s):
    some = q_s.shape[0] // PAIR
    lat = (q_s.shape[1] - 2 * LANES) // 2
    rows = PAIR * some
    turn = place[1] if half == 1 else 1 - place[1]
    lanes = lane_ids((some, LANES))
    for n, q in enumerate((own, other)):
        end = q.shape[0] - 16
        factor = scale_of(as_f32(q[end:, :]))[:1, :1] * (SCALE * LOG2E)
        span = slice(n * some, (n + 1) * some)
        for t in range(lat // LANES):
            at = pl.multiple_of(t * rows + turn * some, some)
            high, low = halves(as_f32(q[pl.ds(at, some), :]) * factor)
            q_s[span, t * LANES : (t + 1) * LANES] = high
            q_s[span, lat + t * LANES : lat + (t + 1) * LANES] = low
        rest = as_f32(q[end - some : end, :]) * factor
        rest = jnp.where(turn == 0, rest, pltpu.roll(rest, LANES // 2, 1))
        high, low = halves(jnp.where(lanes < LANES // 2, rest, 0.0))
        both = high.astype(F32) + pltpu.roll(low.astype(F32), LANES // 2, 1)
        q_s[span, 2 * lat : 2 * lat + LANES] = both.astype(BF16)
        q_s[span, 2 * lat + LANES :] = high


def split_kernel(place, own, other, out):
    load_queries(place, 0, own, other, out)


def split_far(place, own, other, rows, width):
    return pl.pallas_call(
        split_kernel,
        out_shape=jax.ShapeDtypeStruct((rows, width), BF16),
        in_specs=[SMEM, VMEM, VMEM],
        out_specs=VMEM,
        compiler_params=PARAMS,
        cost_estimate=cost(10**7, 4 * 10**6),
        name="split_far",
    )(place, own, other)


def half_kernel(core, values, half, sem):
    some = half.shape[0]
    copy = pltpu.make_async_copy(values.at[pl.ds(core[0] * some, some)], half, sem)
    copy.start()
    copy.wait()


def half_values(core, values):
    heads, lat, vdim = values.shape
    return pl.pallas_call(
        half_kernel,
        out_shape=jax.ShapeDtypeStruct((heads // 2, lat, vdim), BF16),
        in_specs=[SMEM, HBM],
        out_specs=VMEM,
        scratch_shapes=[pltpu.SemaphoreType.DMA],
        compiler_params=pltpu.CompilerParams(vmem_limit_bytes=WHOLE),
        cost_estimate=cost(10**4, 10**6),
        name="half_values",
    )(core, values)


def split_keys(places, arrived, keys_s):
    count = places.shape[0]
    _, part, padded = arrived.shape
    lat = padded - LANES
    rope = lane_ids((part, LANES)) < LANES // 2
    for i in range(count):
        wide = as_f32(arrived[places[i]])
        wide = wide * scale_of(wide[:, lat:])[:, LANES - 1 :]
        span = slice(i * part, (i + 1) * part)
        high, low = halves(wide[:, :lat])
        keys_s[span, :lat] = high
        keys_s[span, lat : 2 * lat] = low
        tail = jnp.where(rope, wide[:, lat:], 0.0)
        keys_s[span, 2 * lat : 2 * lat + LANES] = (tail + pltpu.roll(tail, LANES // 2, 1)).astype(BF16)
        keys_s[span, 2 * lat + LANES :] = halves(tail)[1]


def attend_rows(block_ids, place, half, q, keys_s, vp_own, fetched, passed, out, mixed_s, stat_s):
    heads, lat, vdim = vp_own.shape
    count = block_ids.shape[0]
    part = out.shape[0]
    some = fetched.shape[0]
    keys = keys_s.shape[0]
    lane = lane_ids((1, keys))
    room = jnp.zeros((1, keys), jnp.int32)
    for i in range(count):
        room = jnp.where(lane // part == i, (place[2] - block_ids[i]) * (PAIR * part), room)
    if half == 0:
        room = room + (1 - 2 * place[1]) * part
    room = room - lane % part
    spot = lax.broadcasted_iota(jnp.int32, (q.shape[0], 1), 0) // heads % part
    s = (
        dot_nt(q[:, :lat], keys_s[:, :lat])
        + dot_nt(q[:, lat : 2 * lat], keys_s[:, :lat])
        + dot_nt(q[:, :lat], keys_s[:, lat : 2 * lat])
        + dot_nt(q[:, 2 * lat :], keys_s[:, 2 * lat :])
    )
    s = jnp.where(room + spot >= 0, s, NEG)
    peak = jnp.max(s, axis=-1, keepdims=True)
    p = jnp.exp2(s - peak)
    norm = jnp.sum(p, axis=-1, keepdims=True)
    high, low = halves(p)
    mixed = dot_nn(high, keys_s[:, :lat]) + dot_nn(high, keys_s[:, lat : 2 * lat]) + dot_nn(low, keys_s[:, :lat])
    mixed = mixed / norm
    for t in range(lat // LANES):
        mixed_s[t] = mixed[:, t * LANES : (t + 1) * LANES]
    stat_s[...] = jnp.broadcast_to((peak + jnp.log2(norm)) * 2.0, stat_s.shape)
    results, stats = [], []
    for n in range(PAIR * heads):
        head = n if n < heads else heads * part + ((n - heads) // some + place[0]) % 2 * some + n % some
        rows = pl.ds(head, part, stride=heads)
        high, low = halves(jnp.concatenate([mixed_s[t, rows, :] for t in range(lat // LANES)], axis=-1))
        maps = vp_own[n] if n < heads else (fetched[n - heads] if n < heads + some else passed[n - heads - some])
        both = dot_nn(jnp.concatenate([high, low], axis=0), maps)
        results.append(both[:part] + both[part:])
        stats.append(stat_s[rows, :])
    head_out = jnp.concatenate(results, axis=-1)
    code = row_code(row_peak(head_out))
    inner = head_out.shape[-1]
    coded = as_s16(to_int(head_out, code))
    half = inner // PAIR
    width = some * vdim
    out[:, :half] = coded[:, :half]
    for n, turn in enumerate((place[0], 1 - place[0])):
        at = pl.multiple_of(half + turn * width, width)
        out[:, pl.ds(at, width)] = coded[:, half + n * width : half + (n + 1) * width]
    lane = lane_ids((part, LANES))
    tail = code
    for n in range(PAIR * heads):
        at = n
        if n >= heads:
            turn = place[0] if n < heads + some else 1 - place[0]
            at = heads + turn * some + n % some
        coarse = jnp.floor(stats[n])
        tail = jnp.where(lane == at, coarse, tail)
        tail = jnp.where(lane == at + PAIR * heads, (stats[n] - coarse) * 32767.0, tail)
    out[:, inner:] = as_s16(tail)


def far_kernel(
    places, block_ids, place, q, arrived, vp_own, fetched, passed, out, keys_s, mixed_s, stat_s
):
    split_keys(places, arrived, keys_s)
    attend_rows(block_ids, place, 0, q, keys_s, vp_own, fetched, passed, out, mixed_s, stat_s)


def near_kernel(block_ids, place, own, other, keys_s, vp_own, fetched, passed, out, q_s, mixed_s, stat_s):
    load_queries(place, 1, own, other, q_s)
    attend_rows(block_ids, place, 1, q_s, keys_s, vp_own, fetched, passed, out, mixed_s, stat_s)


def attend_far(places, block_ids, place, q, arrived, vp_own, fetched, passed):
    count = places.shape[0]
    _, part, padded = arrived.shape
    heads, lat, vdim = vp_own.shape
    rows = PAIR * heads * part
    return pl.pallas_call(
        far_kernel,
        out_shape=(
            jax.ShapeDtypeStruct((part, PAIR * heads * vdim + LANES), S16),
            jax.ShapeDtypeStruct((count * part, 2 * padded), BF16),
        ),
        in_specs=[SMEM, SMEM, SMEM] + [VMEM] * 5,
        out_specs=(VMEM, VMEM),
        scratch_shapes=[
            pltpu.VMEM((lat // LANES, rows, LANES), F32),
            pltpu.VMEM((rows, LANES), F32),
        ],
        compiler_params=PARAMS,
        cost_estimate=cost(4 * 10**9, 6 * 10**6, 10**6),
        name="attend_far",
    )(places, block_ids, place, q, arrived, vp_own, fetched, passed)


def attend_near(block_ids, place, own, other, keys, vp_own, fetched, passed, part):
    heads, lat, vdim = vp_own.shape
    rows = PAIR * heads * part
    return pl.pallas_call(
        near_kernel,
        out_shape=jax.ShapeDtypeStruct((part, PAIR * heads * vdim + LANES), S16),
        in_specs=[SMEM, SMEM, VMEM, VMEM, VMEM, VMEM, VMEM, VMEM],
        out_specs=VMEM,
        scratch_shapes=[
            pltpu.VMEM((rows, keys.shape[1]), BF16),
            pltpu.VMEM((lat // LANES, rows, LANES), F32),
            pltpu.VMEM((rows, LANES), F32),
        ],
        compiler_params=PARAMS,
        cost_estimate=cost(4 * 10**9, 6 * 10**6, 10**6),
        name="attend_near",
    )(block_ids, place, own, other, keys, vp_own, fetched, passed)


def merge_kernel(place, here, there, out, *, heads):
    rows, padded = here.shape
    inner = padded - LANES
    width = inner // PAIR
    vdim = width // heads
    tails = [as_f32(x[:, inner:]) for x in (here, there)]
    logs = [(x + pltpu.roll(x, LANES - PAIR * heads, 1) * (1.0 / 32767.0)) * 0.5 for x in tails]
    scales = [scale_of(x)[:, LANES - 1 :] for x in tails]
    merged = []
    for g in range(PAIR):
        a = logs[0] if g == 0 else pltpu.roll(logs[0], LANES - heads, 1)
        b = logs[1] if g == 1 else pltpu.roll(logs[1], LANES - heads, 1)
        top = jnp.maximum(a, b)
        a, b = jnp.exp2(a - top), jnp.exp2(b - top)
        total = a + b
        a, b = a / total * scales[0], b / total * scales[1]
        for h in range(heads):
            x = as_f32(here[:, g * width + h * vdim : g * width + (h + 1) * vdim]) * a[:, h : h + 1]
            y = as_f32(there[:, (1 - g) * width + h * vdim : (1 - g) * width + (h + 1) * vdim]) * b[:, h : h + 1]
            merged.append((x + y).astype(BF16).astype(F32))
    head_out = jnp.concatenate(merged, axis=-1)
    code = row_code(row_peak(head_out))
    coded = as_s16(to_int(head_out, code))
    for g, turn in enumerate((place[1], 1 - place[1])):
        out[:, pl.ds(pl.multiple_of(turn * width, width), width)] = coded[:, g * width : (g + 1) * width]
    out[:, inner:] = as_s16(jnp.broadcast_to(code, (rows, LANES)))


def merge(place, here, there, heads):
    return pl.pallas_call(
        functools.partial(merge_kernel, heads=heads),
        out_shape=jax.ShapeDtypeStruct(here.shape, S16),
        in_specs=[SMEM, VMEM, VMEM],
        out_specs=VMEM,
        compiler_params=PARAMS,
        cost_estimate=cost(10**6, 5 * 10**5),
        name="merge",
    )(place, here, there)


def project_kernel(place, rows_in, near_own, near_other, far_own, far_other, out, wide):
    chips, rows, padded = rows_in.shape
    inner = padded - LANES
    columns, depth = near_own.shape
    core = place[0]
    factor = scale_of(as_f32(rows_in[:, :, inner:]).reshape(chips * rows, LANES))[:, :1]
    sums = [None, None]
    for n, member in enumerate((place[1], 1 - place[1])):
        at = pl.multiple_of(member * depth, depth)
        a = as_f32(rows_in[:, :, pl.ds(at, depth)]).reshape(chips * rows, depth)
        a = (a * factor).astype(BF16)
        for k, weights in enumerate(((near_own, far_own), (near_other, far_other))[n]):
            term = dot_nt(a, weights[...])
            sums[k] = term if n == 0 else sums[k] + term
    spare = 2 * LANES - columns
    keep = LANES - spare
    groups = rows // 8
    for k, at in enumerate((core, 1 - core)):
        wide[:, :columns] = sums[k]
        out[at, :, :rows, :] = wide[:, :LANES].reshape(chips, rows, LANES).astype(BF16)
        rest = wide[:, LANES:].reshape(chips, groups, 8, LANES)
        last = rest[:, groups - 1].reshape(chips * 8, LANES)
        lanes = lane_ids(last.shape)
        packed = []
        for g in range(groups - 1):
            moved = pltpu.roll(last, (keep - spare * g) % LANES, 1)
            packed.append(jnp.where(lanes < keep, rest[:, g].reshape(chips * 8, LANES), moved))
        packed = jnp.concatenate([x.reshape(chips, 8, LANES) for x in packed], axis=1)
        out[at, :, rows:, :] = packed.astype(BF16)


def project(place, rows_in, near_own, near_other, far_own, far_other):
    chips, rows, _ = rows_in.shape
    return pl.pallas_call(
        project_kernel,
        out_shape=jax.ShapeDtypeStruct((2, chips, rows * near_own.shape[0] // LANES, LANES), BF16),
        in_specs=[SMEM] + [VMEM] * 5,
        out_specs=VMEM,
        scratch_shapes=[pltpu.VMEM((chips * rows, 2 * LANES), F32)],
        compiler_params=PARAMS,
        cost_estimate=cost(10**9, 7 * 10**6),
        name="project",
    )(place, rows_in, near_own, near_other, far_own, far_other)


def add_kernel(parts, out):
    cores, outer, groups, packed, _ = parts.shape
    columns, total = out.shape
    rows = total // (cores * groups)
    spare = 2 * LANES - columns
    keep = LANES - spare
    lanes = lane_ids((8, LANES))
    left, right = [], []
    for k in range(cores):
        for g in range(groups):
            full = parts[k, 0, g].astype(F32)
            for z in range(1, outer):
                full = full + parts[k, z, g].astype(F32)
            left.append(full[:rows])
            pieces = [full[rows + 8 * n : rows + 8 * (n + 1)] for n in range(rows // 8 - 1)]
            last = jnp.zeros((8, LANES), F32)
            for n, piece in enumerate(pieces):
                moved = pltpu.roll(piece, (spare * n - keep) % LANES, 1)
                last = jnp.where((lanes >= spare * n) & (lanes < spare * (n + 1)), moved, last)
            right.extend(pieces + [last])
    out[:LANES, :] = jnp.concatenate(left, axis=0).T.astype(BF16)
    out[LANES:, :] = jnp.concatenate(right, axis=0).T[: columns - LANES].astype(BF16)


def add_parts(parts, columns):
    cores, _, groups, packed, _ = parts.shape
    rows = packed * LANES // columns
    return pl.pallas_call(
        add_kernel,
        out_shape=jax.ShapeDtypeStruct((columns, cores * groups * rows), BF16),
        in_specs=[VMEM],
        out_specs=VMEM,
        compiler_params=PARAMS,
        cost_estimate=cost(10**6, 10**6),
        name="add_parts",
    )(parts)


def on_device(queries, latent, selected, value_proj, out_proj):
    plane = ("x", "y", "core")
    ctx_count = lax.axis_size(plane)
    ctx_index = lax.axis_index(plane)
    core = lax.axis_index("core").astype(jnp.int32)
    member = lax.axis_index("zb").astype(jnp.int32)
    block, heads, width = queries.shape
    per_owner = latent.shape[0] // block
    key_blocks = per_owner * ctx_count
    padded = -(-width // LANES) * LANES
    columns = out_proj.shape[1]
    part = block // PAIR
    swap = [(0, 1), (1, 0)]

    parcels = make_parcels(ctx_index[None].astype(jnp.int32), member[None], selected, latent.T, per_owner, part, padded, lax.axis_size("x"))
    parcels, queries, value_near = lax.optimization_barrier((parcels, queries, value_proj))
    arrived = lax.all_to_all(parcels, ("y", "core", "x"), split_axis=0, concat_axis=0, tiled=True)

    q = queries.reshape(block * heads, width)
    near_own = out_proj.T
    q_own = pack_queries(q)
    q_other = lax.ppermute(q_own, "zb", swap)
    near_own = lax.optimization_barrier((q_own, near_own))[1]
    far_own = lax.ppermute(near_own, "core", swap)
    place = jnp.stack([core, member, key_blocks - ctx_count + ctx_index]).astype(jnp.int32)

    fetched = lax.ppermute(half_values(core[None], value_near), "zb", swap)
    passed = lax.ppermute(fetched, "core", swap)
    listed = lax.optimization_barrier((fetched, selected))[1]
    own_list = lax.dynamic_slice_in_dim(listed, ctx_index, 1, 0)[0]
    owner = own_list // per_owner
    second = jnp.any((owner[None, :] == owner[:, None]) & (own_list[None, :] < own_list[:, None]), axis=1)
    places = place_of(owner, ctx_count, lax.axis_size("x")) * 2 + second.astype(jnp.int32)

    slab = lax.optimization_barrier((fetched, near_own))[1]
    near_other = lax.ppermute(slab, "zb", swap)
    arrived = arrived.reshape(2 * ctx_count, part, padded)
    arrived, q_own, q_other = lax.optimization_barrier((arrived, q_own, q_other))
    q_far = split_far(place, q_own, q_other, heads * block, 2 * padded)
    for_partner, keys = attend_far(places, own_list, place, q_far, arrived, value_proj, fetched, passed)
    for_partner, near_other = lax.optimization_barrier((for_partner, near_other))
    there = lax.ppermute(for_partner, "zb", swap)
    far_other = lax.ppermute(near_other, "core", swap)
    here = attend_near(own_list, place, q_own, q_other, keys, value_proj, fetched, passed, part)
    gathered = lax.all_gather(merge(place, here, there, heads), ("x", "y"), axis=0, tiled=False)
    partial = project(place, gathered, near_own, near_other, far_own, far_other)
    partial = partial.reshape(-1, *partial.shape[2:])
    sent = lax.all_to_all(partial, ("core", "zq", "zb"), split_axis=0, concat_axis=0, tiled=True)
    return add_parts(sent.reshape(2, -1, PAIR, *sent.shape[1:]), columns).T


def solution(mesh):
    shape = (4, 4, 2, mesh.shape["head"] // PAIR, PAIR)
    fine = Mesh(mesh.devices.reshape(shape), ("x", "y", "core", "zq", "zb"))
    ctx, head = ("x", "y", "core"), ("zq", "zb")
    in_specs = (
        P(ctx, head, None),
        P(ctx, None),
        P(),
        P(head, None, None),
        P(head, ctx),
    )
    return jax.shard_map(on_device, mesh=fine, in_specs=in_specs, out_specs=P(head, ctx), check_vma=False)
```
